128 devices in a mesh: dp: 8 (over x, core), fsdp: 16 (over y, z).
Axes of the slice: x: 4, y: 4, z: 4, core: 2. Of those that a mesh axis runs over, the one named last changes fastest.
Arguments:
- activations: bfloat16 [1024, 8192], P('dp'), may hold values from -6 to 6
- out_grads: bfloat16 [2, 1024, 22016], P(None, 'dp'), may hold values from -4 to 4
- bases: bfloat16 [2, 8192, 1024], P(None, 'fsdp'), may hold values from -0.0625 to 0.0625
- first_moment: float32 [2, 1024, 22016], P(None, 'fsdp', 'dp'), may hold values from -6 to 6
- second_moment: float32 [2, 1024, 22016], P(None, 'fsdp', 'dp'), may hold values from 0.5 to 8
Outputs:
- weight_update: bfloat16 [2, 8192, 22016], P(None, 'fsdp', 'dp')
- new_first: float32 [2, 1024, 22016], P(None, 'fsdp', 'dp')
- new_second: float32 [2, 1024, 22016], P(None, 'fsdp', 'dp')
The draws below stay inside these ranges and needn't reach their ends.
All inputs are finite; a program needn't handle non-finite values.
Results may differ from the reference program's by a relative error of at most 0.02.
Values may be sent and summed in bfloat16 or wider, within the bound.
No kernel may reach another device: no remote copies, remote signals or barrier semaphores. Data moves between devices by JAX's collectives and lax.ppermute only.
A program may use at most 192 MiB of HBM per device.

```python
import math
import jax
import jax.numpy as jnp
from jax import lax

D = 8192
FF = 22016
R = 1024
TOK_DEV = 128
TOKENS = 1024
N_DP = 8


def spiked(result, own_key, source, target, shards_of, factor):
    owner, partner = [(jnp.arange(result.shape[position]) // (result.shape[position] // shards_of)).reshape([-1 if axis == position else 1 for axis in range(result.ndim)]) for position in (source, target)]
    chosen = jax.random.permutation(own_key, shards_of)[partner]
    strong = (owner == chosen) | (owner == (partner + shards_of // 2) % shards_of)
    return jnp.where(strong, factor * result, result)


def block_scale(stream_key, extent, split, smallest, top_value):
    loudness, own = 1.0, jax.random.fold_in(stream_key, 6)
    for axis_at, blocks in split:
        draws = jnp.exp(jax.random.uniform(jax.random.fold_in(own, axis_at), (blocks,), jnp.float32, smallest / len(split), top_value / len(split)))
        loudness = loudness * jnp.repeat(draws, extent[axis_at] // blocks).reshape([-1 if axis == axis_at else 1 for axis in range(len(extent))])
    return loudness


def bell_draw(stream_key, shape, width, limit, cuts=(), kind=jnp.bfloat16):
    entries = width * jax.random.normal(stream_key, shape, jnp.float32)
    if cuts:
        entries = entries * block_scale(stream_key, shape, cuts, -0.22, 0.18)
    return jnp.clip(entries, -limit, limit).astype(kind)


def noise_with(own_key, shape, scale, reach, cuts, heavy, dtype=jnp.bfloat16):
    entries = scale * jax.random.normal(own_key, shape, jnp.float32)
    if cuts:
        entries = entries * block_scale(own_key, shape, cuts, -0.22, 0.18)
    return jnp.clip(spiked(entries, jax.random.fold_in(own_key, 3), *heavy), -reach, reach).astype(dtype)


def setup_inputs(seed: int = 0) -> dict:
    streams_of = jax.random.split(jax.random.key(seed), 6)
    return {
        "activations": bell_draw(streams_of[0], (TOKENS, D), 1.0, 6.0, ((0, 8),)),
        "out_grads": noise_with(streams_of[1], (2, TOKENS, FF), 0.5, 4.0, ((1, 8),), (1, 2, 8, 2.0)),
        "bases": bell_draw(streams_of[2], (2, D, R), D ** -0.5, 0.0625, ((1, 16),)),
        "first_moment": bell_draw(streams_of[3], (2, R, FF), 1.0, 6.0, ((1, 16), (2, 8)), jnp.float32),
        "second_moment": jnp.clip(jnp.exp(math.log(8.0) - 2.7725887 * jax.random.uniform(streams_of[4], (2, R, FF), jnp.float32) ** block_scale(streams_of[4], (2, R, FF), ((1, 16), (2, 8)), -0.2, 0.2)), 0.5, 8.0),
    }


def one_matrix(activations, grads_one, basis_one, first_one, second_one):
    projected = jnp.dot(activations, basis_one, preferred_element_type=jnp.float32).astype(jnp.bfloat16)
    proj_blocks = projected.reshape(N_DP, TOK_DEV, R).astype(jnp.float32)
    grad_blocks = grads_one.reshape(N_DP, TOK_DEV, FF).astype(jnp.float32)
    parts = jnp.einsum('gtr,gtf->grf', proj_blocks, grad_blocks).astype(jnp.bfloat16)
    parts = lax.optimization_barrier(parts)
    gradient = lax.optimization_barrier(jnp.sum(parts.astype(jnp.float32), axis=0))
    new_first = 0.9 * first_one + 0.1 * gradient
    new_second = 0.999 * second_one + 0.001 * gradient * gradient
    first_fix = 1.0 - 0.9 ** 1000.0
    second_fix = 1.0 - 0.999 ** 1000.0
    direction = (new_first / first_fix / (jnp.sqrt(new_second / second_fix) + 1e-08)).astype(jnp.bfloat16)
    update = jnp.dot(basis_one, direction, preferred_element_type=jnp.float32).astype(jnp.bfloat16)
    return (update, new_first, new_second)

def reference(activations, out_grads, bases, first_moment, second_moment):
    updates = []
    firsts = []
    seconds = []
    for which in range(2):
        update, new_first, new_second = one_matrix(activations, out_grads[which], bases[which], first_moment[which], second_moment[which])
        updates.append(update)
        firsts.append(new_first)
        seconds.append(new_second)
    return (jnp.stack(updates), jnp.stack(firsts), jnp.stack(seconds))
```

```python
import jax
import jax.numpy as jnp
from jax import lax
from jax.experimental import pallas as pl
from jax.experimental.pallas import tpu as pltpu
from jax.sharding import Mesh, PartitionSpec as P

BF16 = jnp.bfloat16
F32 = jnp.float32
SIDE = 4
VMEM = 56 * 1024 * 1024


def receive(value, axis, distance):
    return lax.ppermute(value, axis, [((i + distance) % SIDE, i) for i in range(SIDE)])


def send(value, axis, distance):
    return receive(value, axis, -distance)


def swap_cores(value):
    return lax.ppermute(value, "c", [(0, 1), (1, 0)])


def partial_kernel(where_ref, proj_ref, grads_ref, mine_ref, other_ref):
    half = mine_ref.shape[2]
    both = lax.dot_general(
        proj_ref[...], grads_ref[0], (((0,), (0,)), ((), ())), preferred_element_type=F32
    ).astype(BF16)
    low, high = both[:, :half], both[:, half:]

    @pl.when(where_ref[1] == 0)
    def _():
        mine_ref[0] = low
        other_ref[0] = high

    @pl.when(where_ref[1] == 1)
    def _():
        mine_ref[0] = high
        other_ref[0] = low


def partial_grads(where, proj, grads, which):
    tokens, rank_part = proj.shape
    pair = grads.shape[2] // SIDE
    out = jax.ShapeDtypeStruct((SIDE, rank_part, pair // 2), BF16)
    return pl.pallas_call(
        partial_kernel,
        grid_spec=pltpu.PrefetchScalarGridSpec(
            num_scalar_prefetch=1,
            grid=(SIDE,),
            in_specs=[
                pl.BlockSpec((tokens, rank_part), lambda i, w: (0, 0)),
                pl.BlockSpec((1, tokens, pair), lambda i, w: (which, 0, (w[0] + i) % SIDE)),
            ],
            out_specs=[pl.BlockSpec((1, rank_part, pair // 2), lambda i, w: (i, 0, 0))] * 2,
        ),
        out_shape=[out, out],
        compiler_params=pltpu.CompilerParams(vmem_limit_bytes=VMEM),
        cost_estimate=pl.CostEstimate(
            flops=2 * tokens * rank_part * pair * SIDE,
            bytes_accessed=2 * tokens * pair * SIDE + 2 * rank_part * pair * SIDE,
            transcendentals=0,
        ),
    )(where, proj, grads)


def expand_kernel(*refs):
    columns_a, columns_b = refs[0], refs[1]
    pieces_a, pieces_b = refs[2:7], refs[7:12]
    out_ref = refs[-1]
    base = 0
    for columns, pieces in ((columns_a, pieces_a), (columns_b, pieces_b)):
        width = pieces[0].shape[1]
        for low in range(0, width, 256):
            high = min(low + 256, width)
            total, at = None, 0
            for piece in pieces:
                depth = piece.shape[0]
                term = jnp.dot(
                    columns[0, :, at : at + depth], piece[:, low:high], preferred_element_type=F32
                )
                total = term if total is None else total + term
                at += depth
            out_ref[0, :, base + low : base + high] = total.astype(BF16)
        base += width


def expand(columns_a, columns_b, pieces_a, pieces_b, which, before=None):
    _, rows, ranks = columns_a.shape
    width = pieces_a[0].shape[1] + pieces_b[0].shape[1]
    tile = 256
    pieces = [*pieces_a, *pieces_b]
    in_specs = [pl.BlockSpec((1, tile, ranks), lambda i: (which, i, 0))] * 2
    in_specs += [pl.BlockSpec(p.shape, lambda i: (0, 0)) for p in pieces]
    args = [columns_a, columns_b, *pieces]
    aliases = {}
    if before is not None:
        in_specs.append(pl.BlockSpec(memory_space=pl.ANY))
        aliases = {len(args): 0}
        args.append(before)
    return pl.pallas_call(
        expand_kernel,
        grid=(rows // tile,),
        in_specs=in_specs,
        out_specs=pl.BlockSpec((1, tile, width), lambda i: (which, i, 0)),
        out_shape=jax.ShapeDtypeStruct((2, rows, width), BF16),
        input_output_aliases=aliases,
        compiler_params=pltpu.CompilerParams(vmem_limit_bytes=VMEM),
        cost_estimate=pl.CostEstimate(
            flops=2 * rows * ranks * width,
            bytes_accessed=2 * (rows * ranks + ranks * width + rows * width),
            transcendentals=0,
        ),
    )(*args)


def ring_gather(value, first, second):
    row = jnp.concatenate([value] + [receive(value, first, d) for d in (1, 2, 3)], axis=0)
    half = row.shape[0] // 2
    after = receive(row, second, 1)
    before = receive(row, second, -1)
    far_top = receive(after[:half], second, 1)
    far_bottom = receive(before[half:], second, -1)
    return row, after, far_top, far_bottom, before


def on_device(activations, out_grads, bases, first_moment, second_moment):
    x, c, y, z = (lax.axis_index(n) for n in ("x", "c", "y", "z"))
    where = jnp.stack([x, c]).astype(jnp.int32)
    features, ranks = bases.shape[1:]
    part = ranks // (SIDE * SIDE)
    tokens = activations.shape[0]

    column = jnp.arange(ranks)
    slow, fast, inner = column // (SIDE * part), column // part % SIDE, column % part
    source_b = (((y + slow) % SIDE) * SIDE + (z + fast) % SIDE) * part + inner
    source_a = (((y + fast) % SIDE) * SIDE + (z + slow) % SIDE) * part + inner
    place_b = (column[:, None] == source_b[None, :]).astype(BF16)
    place_a = (column[:, None] == source_a[None, :]).astype(BF16)

    own = lax.dynamic_slice_in_dim(activations, (y * SIDE + z) * features, features, 1)
    partial = jnp.einsum("td,kdr->ktr", own, bases, preferred_element_type=F32).astype(BF16)
    partial = jnp.einsum("ktr,rs->kts", partial, place_b, preferred_element_type=F32).astype(BF16)
    for axis in ("y", "z"):
        width = partial.shape[2] // SIDE
        blocks = [partial[:, :, i * width : (i + 1) * width] for i in range(SIDE)]
        total = blocks[0].astype(F32)
        for i in (1, 3, 2):
            total = total + send(blocks[i], axis, i).astype(F32)
        partial = total.astype(BF16)

    columns_a = jnp.einsum("kdr,rs->kds", bases, place_a, preferred_element_type=F32).astype(BF16)
    columns_b = jnp.einsum("kdr,rs->kds", bases, place_b, preferred_element_type=F32).astype(BF16)

    first_fix = 1.0 - 0.9**1000.0
    second_fix = 1.0 - 0.999**1000.0
    firsts, seconds = [], []
    update = None
    for which in range(2):
        mine, other = partial_grads(where, partial[which], out_grads, which)
        other = swap_cores(other)
        sums = [mine[i].astype(F32) + other[i].astype(F32) for i in range(SIDE)]
        gradient = sums[0]
        for i in (1, 3, 2):
            gradient = gradient + send(sums[i].astype(BF16), "x", i).astype(F32)
        new_first = 0.9 * first_moment[which] + 0.1 * gradient
        new_second = 0.999 * second_moment[which] + 0.001 * gradient * gradient
        direction = (
            new_first / first_fix / (jnp.sqrt(new_second / second_fix) + 1e-08)
        ).astype(BF16)
        firsts.append(new_first)
        seconds.append(new_second)
        cut = (direction.shape[1] // 2 + 127) // 128 * 128
        pieces_a = ring_gather(direction[:, :cut], "y", "z")
        pieces_b = ring_gather(direction[:, cut:], "z", "y")
        update = expand(columns_a, columns_b, pieces_a, pieces_b, which, update)
    return update, jnp.stack(firsts), jnp.stack(seconds)


def solution(mesh):
    grid = Mesh(mesh.devices.reshape(4, 2, 4, 4), ("x", "c", "y", "z"))
    dp, fsdp = ("x", "c"), ("y", "z")
    return jax.shard_map(
        on_device,
        mesh=grid,
        in_specs=(
            P(dp, None),
            P(None, dp, None),
            P(None, fsdp, None),
            P(None, fsdp, dp),
            P(None, fsdp, dp),
        ),
        out_specs=(P(None, fsdp, dp), P(None, fsdp, dp), P(None, fsdp, dp)),
        check_vma=False,
    )
```

```python
import jax
import jax.numpy as jnp
from jax import lax
from jax.experimental import pallas as pl
from jax.experimental.pallas import tpu as pltpu
from jax.sharding import Mesh, PartitionSpec as P

BF16 = jnp.bfloat16
F32 = jnp.float32
SIDE = 4
LANES = 128
VMEM = 56 * 1024 * 1024
PARAMS = pltpu.CompilerParams(vmem_limit_bytes=VMEM)
ANYWHERE = pl.BlockSpec(memory_space=pl.ANY)


def receive(value, axis, distance):
    return lax.ppermute(value, axis, [((i + distance) % SIDE, i) for i in range(SIDE)])


def send(value, axis, distance):
    return receive(value, axis, -distance)


def swap_cores(value):
    return lax.ppermute(value, "c", [(0, 1), (1, 0)])


def cost(flops, moved):
    return pl.CostEstimate(flops=flops, bytes_accessed=moved, transcendentals=0)


def arrange_kernel(where_ref, bases_ref, _, by_y_ref, by_z_ref):
    y, z = where_ref[2], where_ref[3]
    ranks = bases_ref.shape[2]
    part = ranks // (SIDE * SIDE)
    block = ranks // SIDE
    for out_ref, y_outer in ((by_y_ref, True), (by_z_ref, False)):
        for low in range(0, ranks, block):
            source = lax.broadcasted_iota(jnp.int32, (ranks, block), 0)
            column = lax.broadcasted_iota(jnp.int32, (ranks, block), 1) + low
            outer, inner = column // (SIDE * part), (column // part) & (SIDE - 1)
            dy, dz = (outer, inner) if y_outer else (inner, outer)
            wanted = (((y + dy) & (SIDE - 1)) * SIDE + ((z + dz) & (SIDE - 1))) * part
            wanted = wanted + (column & (part - 1))
            place = jnp.where(source == wanted, 1.0, 0.0).astype(BF16)
            for k in range(bases_ref.shape[0]):
                out_ref[k, :, low : low + block] = jnp.dot(
                    bases_ref[k], place, preferred_element_type=F32
                ).astype(BF16)


def arrange(where, bases, after):
    out = jax.ShapeDtypeStruct(bases.shape, BF16)
    whole = pl.BlockSpec(bases.shape, lambda i, w: (0, 0, 0))
    return pl.pallas_call(
        arrange_kernel,
        grid_spec=pltpu.PrefetchScalarGridSpec(
            num_scalar_prefetch=1, grid=(1,), in_specs=[whole, ANYWHERE], out_specs=[whole] * 2
        ),
        out_shape=[out, out],
        compiler_params=PARAMS,
        cost_estimate=cost(4 * bases.size * bases.shape[2], 6 * bases.size),
    )(where, bases, after)


def partial_kernel(where_ref, proj_ref, grads_ref, _, mine_ref, other_ref):
    half = mine_ref.shape[2]
    both = lax.dot_general(
        proj_ref[...], grads_ref[0], (((0,), (0,)), ((), ())), preferred_element_type=F32
    ).astype(BF16)
    low, high = both[:, :half], both[:, half:]

    @pl.when(where_ref[1] == 0)
    def _():
        mine_ref[0] = low
        other_ref[0] = high

    @pl.when(where_ref[1] == 1)
    def _():
        mine_ref[0] = high
        other_ref[0] = low


def partial_grads(where, proj, grads, which, after):
    tokens, rank_part = proj.shape
    pair = grads.shape[2] // SIDE
    out = jax.ShapeDtypeStruct((SIDE, rank_part, pair // 2), BF16)
    return pl.pallas_call(
        partial_kernel,
        grid_spec=pltpu.PrefetchScalarGridSpec(
            num_scalar_prefetch=1,
            grid=(SIDE,),
            in_specs=[
                pl.BlockSpec((tokens, rank_part), lambda i, w: (0, 0)),
                pl.BlockSpec((1, tokens, pair), lambda i, w: (which, 0, (w[0] + i) % SIDE)),
                ANYWHERE,
            ],
            out_specs=[pl.BlockSpec((1, rank_part, pair // 2), lambda i, w: (i, 0, 0))] * 2,
        ),
        out_shape=[out, out],
        compiler_params=PARAMS,
        cost_estimate=cost(
            2 * tokens * rank_part * pair * SIDE, 2 * tokens * pair * SIDE + 2 * rank_part * pair * SIDE
        ),
    )(where, proj, grads, after)


def direction_kernel(*refs):
    mine_ref, other_ref, one_ref, two_ref, first_ref, second_ref = refs[:6]
    new_first_ref, new_second_ref, left_ref, right_ref = refs[-4:]
    gradient = mine_ref[0].astype(F32) + other_ref[0].astype(F32)
    gradient = gradient + one_ref[...].astype(F32) + two_ref[...].astype(F32)
    new_first = 0.9 * first_ref[0] + 0.1 * gradient
    new_second = 0.999 * second_ref[0] + 0.001 * gradient * gradient
    new_first_ref[0] = new_first
    new_second_ref[0] = new_second
    first_fix = 1.0 - 0.9**1000.0
    second_fix = 1.0 - 0.999**1000.0
    direction = (new_first / first_fix / (jnp.sqrt(new_second / second_fix) + 1e-08)).astype(BF16)
    cut = left_ref.shape[1]
    rest = direction.shape[1] - cut
    left_ref[...] = direction[:, :cut]
    right_ref[:, :rest] = direction[:, cut:]
    right_ref[:, rest:] = jnp.zeros((right_ref.shape[0], cut - rest), BF16)


def directions(mine, other, one, two, first_moment, second_moment, which, before):
    _, rows, width = first_moment.shape
    cut = (width // 2 + LANES - 1) // LANES * LANES
    tile = 16
    zero = pl.BlockSpec((1, tile, width), lambda i: (0, i, 0))
    flat = pl.BlockSpec((tile, width), lambda i: (i, 0))
    own = pl.BlockSpec((1, tile, width), lambda i: (which, i, 0))
    half = pl.BlockSpec((tile, cut), lambda i: (i, 0))
    in_specs = [zero, zero, flat, flat, own, own]
    args = [mine, other, one, two, first_moment, second_moment]
    aliases = {}
    if before:
        aliases = {len(args) + i: i for i in range(len(before))}
        in_specs += [ANYWHERE] * len(before)
        args += before
    piece = jax.ShapeDtypeStruct((rows, cut), BF16)
    full = jax.ShapeDtypeStruct(first_moment.shape, F32)
    return pl.pallas_call(
        direction_kernel,
        grid=(rows // tile,),
        in_specs=in_specs,
        out_specs=[own, own, half, half],
        out_shape=[full, full, piece, piece],
        input_output_aliases=aliases,
        compiler_params=PARAMS,
        cost_estimate=cost(30 * rows * width, 26 * rows * width),
    )(*args)


def stack_kernel(*refs):
    rows = refs[0].shape[0]
    for i, ref in enumerate(refs[:-1]):
        refs[-1][i * rows : (i + 1) * rows, :] = ref[...]


def stack(pieces):
    rows, width = pieces[0].shape
    return pl.pallas_call(
        stack_kernel,
        out_shape=jax.ShapeDtypeStruct((rows * len(pieces), width), BF16),
        compiler_params=PARAMS,
        cost_estimate=cost(0, 4 * rows * width * len(pieces)),
    )(*pieces)


def expand_kernel(columns_ref, *refs):
    pieces, out_ref = refs[:SIDE], refs[-1]
    width = pieces[0].shape[1]
    for low in range(0, width, 256):
        high = min(low + 256, width)
        total, at = None, 0
        for piece in pieces:
            depth = piece.shape[0]
            term = jnp.dot(
                columns_ref[0, :, at : at + depth], piece[:, low:high], preferred_element_type=F32
            )
            total = term if total is None else total + term
            at += depth
        out_ref[0, low:high, :] = total.T.astype(BF16)


def expand(columns, pieces, width, which, place, before):
    count, rows, ranks = columns.shape
    cut = pieces[0].shape[1]
    in_specs = [pl.BlockSpec((1, rows, ranks), lambda i: (which, 0, 0))]
    in_specs += [pl.BlockSpec(p.shape, lambda i: (0, 0)) for p in pieces]
    args = [columns, *pieces]
    aliases = {}
    if before is not None:
        in_specs.append(ANYWHERE)
        aliases = {len(args): 0}
        args.append(before)
    return pl.pallas_call(
        expand_kernel,
        grid=(1,),
        in_specs=in_specs,
        out_specs=pl.BlockSpec((1, cut, rows), lambda i: (which, place, 0)),
        out_shape=jax.ShapeDtypeStruct((count, width, rows), BF16),
        input_output_aliases=aliases,
        compiler_params=PARAMS,
        cost_estimate=cost(2 * rows * ranks * cut, 2 * (rows * ranks + ranks * cut + rows * cut)),
    )(*args)


def ring_gather(value, first, second, way):
    row = stack([value] + [receive(value, first, d) for d in (1, 2, 3)])
    after = receive(row, second, 1)
    before = receive(row, second, -1)
    far = receive(after if way == 1 else before, second, way)
    return row, after, far, before


def on_device(activations, out_grads, bases, first_moment, second_moment):
    where = jnp.stack([lax.axis_index(n) for n in ("x", "c", "y", "z")]).astype(jnp.int32)
    y, z = where[2], where[3]
    features, ranks = bases.shape[1:]
    part = ranks // (SIDE * SIDE)
    width = first_moment.shape[2]

    column = jnp.arange(ranks)
    slow, fast, inner = column // (SIDE * part), column // part % SIDE, column % part
    source = (((y + slow) % SIDE) * SIDE + (z + fast) % SIDE) * part + inner
    place = (column[:, None] == source[None, :]).astype(BF16)
    own = lax.dynamic_slice_in_dim(activations, (y * SIDE + z) * features, features, 1)
    partial = jnp.einsum("td,kdr->ktr", own, bases, preferred_element_type=F32).astype(BF16)
    partial = jnp.einsum("ktr,rs->kts", partial, place, preferred_element_type=F32).astype(BF16)
    first_sent = None
    for axis in ("y", "z"):
        size = partial.shape[2] // SIDE
        blocks = [partial[:, :, i * size : (i + 1) * size] for i in range(SIDE)]
        first_sent = blocks[2] if first_sent is None else first_sent
        total = blocks[0].astype(F32)
        for i in (1, 3, 2):
            total = total + send(blocks[i], axis, i).astype(F32)
        partial = total.astype(BF16)
    columns_y, columns_z = arrange(where, bases, first_sent)

    moments, update = [], None
    after = columns_y
    for which in range(2):
        way = 1 if which == 0 else -1
        mine, other = partial_grads(where, partial[which], out_grads, which, after)
        other = swap_cores(other)
        sums = [mine[i].astype(F32) + other[i].astype(F32) for i in range(SIDE)]
        near = send(sums[-way % SIDE].astype(BF16), "x", -way)
        far = sums[2].astype(BF16)
        after = far
        passed = send(far, "x", way).astype(F32) + sums[way % SIDE]
        passed = send(passed.astype(BF16), "x", way)
        *moments, left, right = directions(
            mine, other, near, passed, first_moment, second_moment, which, moments
        )
        for half, first, second, columns in (
            (0, "y", "z", columns_z),
            (1, "z", "y", columns_y),
        ):
            pieces = ring_gather((left, right)[half], first, second, way)
            update = expand(columns, pieces, width, which, half, update)
    return jnp.swapaxes(update, 1, 2), *moments


def solution(mesh):
    grid = Mesh(mesh.devices.reshape(4, 2, 4, 4), ("x", "c", "y", "z"))
    dp, fsdp = ("x", "c"), ("y", "z")
    return jax.shard_map(
        on_device,
        mesh=grid,
        in_specs=(
            P(dp, None),
            P(None, dp, None),
            P(None, fsdp, None),
            P(None, fsdp, dp),
            P(None, fsdp, dp),
        ),
        out_specs=(P(None, fsdp, dp), P(None, fsdp, dp), P(None, fsdp, dp)),
        check_vma=False,
    )
```

```python
import functools

import jax
import jax.numpy as jnp
from jax import lax
from jax.experimental import pallas as pl
from jax.experimental.pallas import tpu as pltpu
from jax.sharding import Mesh, PartitionSpec as P

BF16 = jnp.bfloat16
F32 = jnp.float32
SIDE = 4
LANES = 128
VMEM = 56 * 1024 * 1024
PARAMS = pltpu.CompilerParams(vmem_limit_bytes=VMEM)
ANYWHERE = pl.BlockSpec(memory_space=pl.ANY)


def receive(value, axis, distance):
    return lax.ppermute(value, axis, [((i + distance) % SIDE, i) for i in range(SIDE)])


def send(value, axis, distance):
    return receive(value, axis, -distance)


def swap_cores(value):
    return lax.ppermute(value, "c", [(0, 1), (1, 0)])


def held(shape, dtype=BF16):
    return pltpu.HBM(shape, dtype)


def cost(flops, moved):
    return pl.CostEstimate(flops=flops, bytes_accessed=moved, transcendentals=0)


def arrange_kernel(where_ref, bases_ref, _, by_y_ref, by_z_ref):
    y, z = where_ref[2], where_ref[3]
    ranks = bases_ref.shape[2]
    part = ranks // (SIDE * SIDE)
    block = ranks // SIDE
    for out_ref, y_outer in ((by_y_ref, True), (by_z_ref, False)):
        for low in range(0, ranks, block):
            source = lax.broadcasted_iota(jnp.int32, (ranks, block), 0)
            column = lax.broadcasted_iota(jnp.int32, (ranks, block), 1) + low
            outer, inner = column // (SIDE * part), (column // part) & (SIDE - 1)
            dy, dz = (outer, inner) if y_outer else (inner, outer)
            wanted = (((y + dy) & (SIDE - 1)) * SIDE + ((z + dz) & (SIDE - 1))) * part
            wanted = wanted + (column & (part - 1))
            place = jnp.where(source == wanted, 1.0, 0.0).astype(BF16)
            out_ref[:, low : low + block] = jnp.dot(
                bases_ref[0], place, preferred_element_type=F32
            ).astype(BF16)


def arrange(where, bases, which, after):
    _, rows, ranks = bases.shape
    return pl.pallas_call(
        arrange_kernel,
        grid_spec=pltpu.PrefetchScalarGridSpec(
            num_scalar_prefetch=1,
            grid=(1,),
            in_specs=[pl.BlockSpec((1, rows, ranks), lambda i, w: (which, 0, 0)), ANYWHERE],
            out_specs=[pl.BlockSpec((rows, ranks), lambda i, w: (0, 0))] * 2,
        ),
        out_shape=[held((rows, ranks))] * 2,
        compiler_params=PARAMS,
        cost_estimate=cost(4 * rows * ranks * ranks, 6 * rows * ranks),
    )(where, bases, after)


def partial_kernel(where_ref, proj_ref, grads_ref, _, mine_ref, other_ref):
    half = mine_ref.shape[2]
    both = lax.dot_general(
        proj_ref[...], grads_ref[0], (((0,), (0,)), ((), ())), preferred_element_type=F32
    ).astype(BF16)
    low, high = both[:, :half], both[:, half:]

    @pl.when(where_ref[1] == 0)
    def _():
        mine_ref[0] = low
        other_ref[0] = high

    @pl.when(where_ref[1] == 1)
    def _():
        mine_ref[0] = high
        other_ref[0] = low


def partial_grads(where, proj, grads, which, after):
    tokens, rank_part = proj.shape
    pair = grads.shape[2] // SIDE
    out = held((SIDE, rank_part, pair // 2))
    return pl.pallas_call(
        partial_kernel,
        grid_spec=pltpu.PrefetchScalarGridSpec(
            num_scalar_prefetch=1,
            grid=(SIDE,),
            in_specs=[
                pl.BlockSpec((tokens, rank_part), lambda i, w: (0, 0)),
                pl.BlockSpec((1, tokens, pair), lambda i, w: (which, 0, (w[0] + i) % SIDE)),
                ANYWHERE,
            ],
            out_specs=[pl.BlockSpec((1, rank_part, pair // 2), lambda i, w: (i, 0, 0))] * 2,
        ),
        out_shape=[out, out],
        compiler_params=PARAMS,
        cost_estimate=cost(
            2 * tokens * rank_part * pair * SIDE, 2 * tokens * pair * SIDE + 2 * rank_part * pair * SIDE
        ),
    )(where, proj, grads, after)


def sums_kernel(mine_ref, other_ref, near_ref, far_ref, via_ref, *, order):
    for i, ref in zip(order, (near_ref, far_ref, via_ref)):
        total = mine_ref[i].astype(F32) + other_ref[i].astype(F32)
        ref[...] = total.astype(ref.dtype)


def sums(mine, other, order):
    _, rows, width = mine.shape
    return pl.pallas_call(
        functools.partial(sums_kernel, order=order),
        out_shape=[held((rows, width)), held((rows, width)), held((rows, width), F32)],
        compiler_params=PARAMS,
        cost_estimate=cost(3 * rows * width, 20 * rows * width),
    )(mine, other)


def relay_kernel(one_ref, two_ref, _, out_ref):
    out_ref[...] = (one_ref[...].astype(F32) + two_ref[...]).astype(BF16)


def relay(one, two, after):
    rows, width = one.shape
    whole = pl.BlockSpec((rows, width), lambda: (0, 0))
    return pl.pallas_call(
        relay_kernel,
        in_specs=[whole, whole, ANYWHERE],
        out_specs=whole,
        out_shape=held((rows, width)),
        compiler_params=PARAMS,
        cost_estimate=cost(rows * width, 8 * rows * width),
    )(one, two, after)


def direction_kernel(*refs, pieces):
    mine_ref, other_ref, one_ref, two_ref, first_ref, second_ref = refs[:6]
    new_first_ref, new_second_ref = refs[-2 - pieces : -pieces]
    gradient = mine_ref[0].astype(F32) + other_ref[0].astype(F32)
    gradient = gradient + one_ref[...].astype(F32) + two_ref[...].astype(F32)
    new_first = 0.9 * first_ref[0] + 0.1 * gradient
    new_second = 0.999 * second_ref[0] + 0.001 * gradient * gradient
    new_first_ref[0] = new_first
    new_second_ref[0] = new_second
    first_fix = 1.0 - 0.9**1000.0
    second_fix = 1.0 - 0.999**1000.0
    direction = (new_first / first_fix / (jnp.sqrt(new_second / second_fix) + 1e-08)).astype(BF16)
    low = 0
    for ref in refs[-pieces:]:
        size = min(ref.shape[1], direction.shape[1] - low)
        ref[:, :size] = direction[:, low : low + size]
        if size < ref.shape[1]:
            ref[:, size:] = jnp.zeros((ref.shape[0], ref.shape[1] - size), BF16)
        low += size


def directions(mine, other, one, two, first_moment, second_moment, which, pieces, before, after):
    _, rows, width = first_moment.shape
    cut = (width // pieces + LANES - 1) // LANES * LANES
    tile = 16
    zero = pl.BlockSpec((1, tile, width), lambda i: (0, i, 0))
    flat = pl.BlockSpec((tile, width), lambda i: (i, 0))
    own = pl.BlockSpec((1, tile, width), lambda i: (which, i, 0))
    half = pl.BlockSpec((tile, cut), lambda i: (i, 0))
    in_specs = [zero, zero, flat, flat, own, own]
    args = [mine, other, one, two, first_moment, second_moment]
    aliases = {len(args) + i: i for i in range(len(before))}
    args += [*before, after]
    in_specs += [ANYWHERE] * (len(before) + 1)
    piece = held((rows, cut))
    full = jax.ShapeDtypeStruct(first_moment.shape, F32)
    return pl.pallas_call(
        functools.partial(direction_kernel, pieces=pieces),
        grid=(rows // tile,),
        in_specs=in_specs,
        out_specs=[own, own] + [half] * pieces,
        out_shape=[full, full] + [piece] * pieces,
        input_output_aliases=aliases,
        compiler_params=PARAMS,
        cost_estimate=cost(30 * rows * width, 26 * rows * width),
    )(*args)


def stack_kernel(*refs):
    rows = refs[0].shape[0]
    for i, ref in enumerate(refs[:-1]):
        refs[-1][i * rows : (i + 1) * rows, :] = ref[...]


def stack(pieces):
    rows, width = pieces[0].shape
    return pl.pallas_call(
        stack_kernel,
        out_shape=held((rows * len(pieces), width)),
        compiler_params=PARAMS,
        cost_estimate=cost(0, 4 * rows * width * len(pieces)),
    )(*pieces)


def expand_kernel(columns_ref, *refs, count):
    pieces, out_ref = refs[:count], refs[-1]
    width = pieces[0].shape[1]
    for low in range(0, width, 256):
        high = min(low + 256, width)
        total, at = None, 0
        for piece in pieces:
            depth = piece.shape[0]
            term = jnp.dot(
                columns_ref[:, at : at + depth], piece[:, low:high], preferred_element_type=F32
            )
            total = term if total is None else total + term
            at += depth
        out_ref[0, low:high, :] = total.T.astype(BF16)


def expand_half(columns, pieces, which, place, update):
    rows, ranks = columns.shape
    cut = pieces[0].shape[1]
    in_specs = [pl.BlockSpec((rows, ranks), lambda i: (0, 0))]
    in_specs += [pl.BlockSpec(p.shape, lambda i: (0, 0)) for p in pieces]
    return pl.pallas_call(
        functools.partial(expand_kernel, count=len(pieces)),
        grid=(1,),
        in_specs=[*in_specs, ANYWHERE],
        out_specs=pl.BlockSpec((1, cut, rows), lambda i: (which, place, 0)),
        out_shape=jax.ShapeDtypeStruct(update.shape, BF16),
        input_output_aliases={len(in_specs): 0},
        compiler_params=PARAMS,
        cost_estimate=cost(2 * rows * ranks * cut, 2 * (rows * ranks + ranks * cut + rows * cut)),
    )(columns, *pieces, update)


def expand_whole_kernel(bases_ref, gathered_ref, out_ref):
    out_ref[0] = (
        jnp.dot(bases_ref[0], gathered_ref[...], preferred_element_type=F32).T.astype(BF16)
    )


def expand_whole(bases, gathered, which, width):
    count, rows, ranks = bases.shape
    tile = 256
    return pl.pallas_call(
        expand_whole_kernel,
        grid=(gathered.shape[1] // tile,),
        in_specs=[
            pl.BlockSpec((1, rows, ranks), lambda i: (which, 0, 0)),
            pl.BlockSpec((ranks, tile), lambda i: (0, i)),
        ],
        out_specs=pl.BlockSpec((1, tile, rows), lambda i: (which, i, 0)),
        out_shape=jax.ShapeDtypeStruct((count, width, rows), BF16),
        compiler_params=PARAMS,
        cost_estimate=cost(
            2 * rows * ranks * width, 2 * (rows * ranks + ranks * width + rows * width)
        ),
    )(bases, gathered)


def ring_gather(value, first, second):
    row = stack([value] + [receive(value, first, d) for d in (1, 2, 3)])
    half = row.shape[0] // 2
    after = receive(row, second, 1)
    before = receive(row, second, -1)
    far_top = receive(after[:half], second, 1)
    far_bottom = receive(before[half:], second, -1)
    return row, after, far_top, far_bottom, before


def on_device(activations, out_grads, bases, first_moment, second_moment):
    where = jnp.stack([lax.axis_index(n) for n in ("x", "c", "y", "z")]).astype(jnp.int32)
    y, z = where[2], where[3]
    features, ranks = bases.shape[1:]
    part = ranks // (SIDE * SIDE)
    width = first_moment.shape[2]

    column = jnp.arange(ranks)
    slow, fast, inner = column // (SIDE * part), column // part % SIDE, column % part
    source = (((y + slow) % SIDE) * SIDE + (z + fast) % SIDE) * part + inner
    place = (column[:, None] == source[None, :]).astype(BF16)
    own = lax.dynamic_slice_in_dim(activations, (y * SIDE + z) * features, features, 1)
    partial = jnp.einsum("td,kdr->ktr", own, bases, preferred_element_type=F32).astype(BF16)
    partial = jnp.einsum("ktr,rs->kts", partial, place, preferred_element_type=F32).astype(BF16)
    for axis in ("y", "z"):
        size = partial.shape[2] // SIDE
        blocks = [partial[:, :, i * size : (i + 1) * size] for i in range(SIDE)]
        total = blocks[0].astype(F32)
        for i in (1, 3, 2):
            total = total + send(blocks[i], axis, i).astype(F32)
        partial = total.astype(BF16)

    mine, other = partial_grads(where, partial[0], out_grads, 0, where)
    other = swap_cores(other)
    near, far, via = sums(mine, other, (3, 2, 1))
    columns_y, columns_z = arrange(where, bases, 1, far)
    near = send(near, "x", -1)
    passed = relay(send(far, "x", 1), via, columns_y)
    mine_1, other_1 = partial_grads(where, partial[1], out_grads, 1, passed)
    passed = send(passed, "x", 1)
    *moments, whole = directions(
        mine, other, near, passed, first_moment, second_moment, 0, 1, [], mine_1
    )
    gathered = lax.all_gather(whole, ("y", "z"), axis=0, tiled=True)

    other_1 = swap_cores(other_1)
    near, far, via = sums(mine_1, other_1, (1, 2, 3))
    near = send(near, "x", 1)
    passed = send(relay(send(far, "x", -1), via, far), "x", -1)
    *moments, left, right = directions(
        mine_1, other_1, near, passed, first_moment, second_moment, 1, 2, moments, passed
    )
    pieces_left = ring_gather(left, "y", "z")
    pieces_right = ring_gather(right, "z", "y")
    update = expand_whole(bases, gathered, 0, width)
    update = expand_half(columns_z, pieces_left, 1, 0, update)
    update = expand_half(columns_y, pieces_right, 1, 1, update)
    return jnp.swapaxes(update, 1, 2), *moments


def solution(mesh):
    grid = Mesh(mesh.devices.reshape(4, 2, 4, 4), ("x", "c", "y", "z"))
    dp, fsdp = ("x", "c"), ("y", "z")
    return jax.shard_map(
        on_device,
        mesh=grid,
        in_specs=(
            P(dp, None),
            P(None, dp, None),
            P(None, fsdp, None),
            P(None, fsdp, dp),
            P(None, fsdp, dp),
        ),
        out_specs=(P(None, fsdp, dp), P(None, fsdp, dp), P(None, fsdp, dp)),
        check_vma=False,
    )
```

```python
import functools

import jax
import jax.numpy as jnp
from jax import lax
from jax.experimental import pallas as pl
from jax.experimental.pallas import tpu as pltpu
from jax.sharding import Mesh, PartitionSpec as P

BF16 = jnp.bfloat16
F32 = jnp.float32
SIDE = 4
LANES = 128
VMEM = 56 * 1024 * 1024
PARAMS = pltpu.CompilerParams(vmem_limit_bytes=VMEM)
ANYWHERE = pl.BlockSpec(memory_space=pl.ANY)


def receive(value, axis, distance):
    return lax.ppermute(value, axis, [((i + distance) % SIDE, i) for i in range(SIDE)])


def send(value, axis, distance):
    return receive(value, axis, -distance)


def swap_cores(value):
    return lax.ppermute(value, "c", [(0, 1), (1, 0)])


def held(shape, dtype=BF16):
    return pltpu.HBM(shape, dtype)


def cost(flops, moved):
    return pl.CostEstimate(flops=flops, bytes_accessed=moved, transcendentals=0)


def arrange_kernel(where_ref, bases_ref, _, by_y_ref, by_z_ref):
    y, z = where_ref[2], where_ref[3]
    ranks = bases_ref.shape[2]
    part = ranks // (SIDE * SIDE)
    block = ranks // SIDE
    for out_ref, y_outer in ((by_y_ref, True), (by_z_ref, False)):
        for low in range(0, ranks, block):
            source = lax.broadcasted_iota(jnp.int32, (ranks, block), 0)
            column = lax.broadcasted_iota(jnp.int32, (ranks, block), 1) + low
            outer, inner = column // (SIDE * part), (column // part) & (SIDE - 1)
            dy, dz = (outer, inner) if y_outer else (inner, outer)
            wanted = (((y + dy) & (SIDE - 1)) * SIDE + ((z + dz) & (SIDE - 1))) * part
            wanted = wanted + (column & (part - 1))
            place = jnp.where(source == wanted, 1.0, 0.0).astype(BF16)
            out_ref[:, low : low + block] = jnp.dot(
                bases_ref[0], place, preferred_element_type=F32
            ).astype(BF16)


def arrange(where, bases, which, after):
    _, rows, ranks = bases.shape
    return pl.pallas_call(
        arrange_kernel,
        grid_spec=pltpu.PrefetchScalarGridSpec(
            num_scalar_prefetch=1,
            grid=(1,),
            in_specs=[pl.BlockSpec((1, rows, ranks), lambda i, w: (which, 0, 0)), ANYWHERE],
            out_specs=[pl.BlockSpec((rows, ranks), lambda i, w: (0, 0))] * 2,
        ),
        out_shape=[held((rows, ranks))] * 2,
        compiler_params=PARAMS,
        cost_estimate=cost(4 * rows * ranks * ranks, 6 * rows * ranks),
    )(where, bases, after)


def partial_kernel(where_ref, proj_ref, other_proj_ref, grads_ref, other_grads_ref, _, *outs):
    step = pl.program_id(0)
    proj = jnp.concatenate([proj_ref[...], other_proj_ref[...]], axis=0)
    grads = jnp.concatenate([grads_ref[0], other_grads_ref[0]], axis=0)
    total = lax.dot_general(proj, grads, (((0,), (0,)), ((), ())), preferred_element_type=F32)
    span, width = total.shape[1], outs[0].shape[1]
    later = pltpu.roll(total, width, 1)
    total = jnp.where(where_ref[1] == 1, later, total)[:, :width]
    for i, ref in enumerate(outs):

        @pl.when(step == i)
        def _(ref=ref):
            ref[...] = total.astype(ref.dtype)


def partial_grads(where, proj, other_proj, grads, other_grads, which, after):
    tokens, rank_part = proj.shape
    pair = grads.shape[2] // SIDE
    width = pair // 2
    span = (width + LANES - 1) // LANES * LANES
    skip = (pair - span) // LANES

    def window(i, w):
        block = (w[0] + i) & (SIDE - 1)
        return which, 0, pl.multiple_of((block * (pair // LANES) + w[1] * skip) * LANES, LANES)

    small = pl.BlockSpec((tokens, rank_part), lambda i, w: (0, 0))
    large = pl.BlockSpec((pl.Element(1), pl.Element(tokens), pl.Element(span)), window)
    return pl.pallas_call(
        partial_kernel,
        grid_spec=pltpu.PrefetchScalarGridSpec(
            num_scalar_prefetch=1,
            grid=(SIDE,),
            in_specs=[small, small, large, large, ANYWHERE],
            out_specs=[pl.BlockSpec((rank_part, width), lambda i, w: (0, 0))] * SIDE,
        ),
        out_shape=[held((rank_part, width), F32)] + [held((rank_part, width))] * (SIDE - 1),
        compiler_params=PARAMS,
        cost_estimate=cost(
            4 * tokens * rank_part * width * SIDE, 4 * (tokens + rank_part) * width * SIDE
        ),
    )(where, proj, other_proj, grads, other_grads, after)


def direction_kernel(*refs, pieces):
    own_ref, first_ref, second_ref = refs[0], refs[4], refs[5]
    new_first_ref, new_second_ref = refs[-2 - pieces : -pieces]
    gradient = own_ref[...]
    for ref in refs[1:4]:
        gradient = gradient + ref[...].astype(F32)
    new_first = 0.9 * first_ref[0] + 0.1 * gradient
    new_second = 0.999 * second_ref[0] + 0.001 * gradient * gradient
    new_first_ref[0] = new_first
    new_second_ref[0] = new_second
    first_fix = 1.0 - 0.9**1000.0
    second_fix = 1.0 - 0.999**1000.0
    root = jnp.sqrt(new_second * (1.0 / second_fix)) + 1e-08
    direction = (new_first * (1.0 / first_fix) / root).astype(BF16)
    low = 0
    for ref in refs[-pieces:]:
        size = min(ref.shape[1], direction.shape[1] - low)
        ref[:, :size] = direction[:, low : low + size]
        if size < ref.shape[1]:
            ref[:, size:] = jnp.zeros((ref.shape[0], ref.shape[1] - size), BF16)
        low += size


def directions(own_sum, sums, first_moment, second_moment, which, pieces, before, after):
    _, rows, width = first_moment.shape
    cut = (width // pieces + LANES - 1) // LANES * LANES
    tile = 32
    flat = pl.BlockSpec((tile, width), lambda i: (i, 0))
    own = pl.BlockSpec((1, tile, width), lambda i: (which, i, 0))
    half = pl.BlockSpec((tile, cut), lambda i: (i, 0))
    in_specs = [flat] * SIDE + [own, own]
    args = [own_sum, *sums, first_moment, second_moment]
    aliases = {len(args) + i: i for i in range(len(before))}
    args += [*before, after]
    in_specs += [ANYWHERE] * (len(before) + 1)
    piece = held((rows, cut))
    full = jax.ShapeDtypeStruct(first_moment.shape, F32)
    return pl.pallas_call(
        functools.partial(direction_kernel, pieces=pieces),
        grid=(rows // tile,),
        in_specs=in_specs,
        out_specs=[own, own] + [half] * pieces,
        out_shape=[full, full] + [piece] * pieces,
        input_output_aliases=aliases,
        compiler_params=PARAMS,
        cost_estimate=cost(30 * rows * width, 26 * rows * width),
    )(*args)


def stack_kernel(*refs):
    rows = refs[0].shape[0]
    for i, ref in enumerate(refs[:-1]):
        refs[-1][i * rows : (i + 1) * rows, :] = ref[...]


def stack(pieces):
    rows, width = pieces[0].shape
    return pl.pallas_call(
        stack_kernel,
        out_shape=held((rows * len(pieces), width)),
        compiler_params=PARAMS,
        cost_estimate=cost(0, 4 * rows * width * len(pieces)),
    )(*pieces)


def expand_kernel(*refs, counts, which):
    halves = len(counts)
    out_ref, columns, pieces, outs, in_sems, out_sems = refs[-6:]
    cut = pieces.shape[2]
    loads, refs = [], list(refs)
    for half, count in enumerate(counts):
        loads.append([(refs.pop(0), columns.at[half])])
        at = 0
        for _ in range(count):
            ref = refs.pop(0)
            loads[half].append((ref, pieces.at[half, pl.ds(at, ref.shape[0])]))
            at += ref.shape[0]
    copies = [
        [pltpu.make_async_copy(a, b, in_sems.at[half, i]) for i, (a, b) in enumerate(group)]
        for half, group in enumerate(loads)
    ]
    for group in copies:
        for copy in group:
            copy.start()
    stores = []
    for half, group in enumerate(copies):
        for copy in group:
            copy.wait()
        for low in range(0, cut, 256):
            high = min(low + 256, cut)
            total = jnp.dot(columns[half], pieces[half, :, low:high], preferred_element_type=F32)
            outs[half, low:high, :] = total.T.astype(BF16)
        size = min(cut, out_ref.shape[1] - half * cut)
        stores.append(
            pltpu.make_async_copy(
                outs.at[half, pl.ds(0, size)],
                out_ref.at[which, pl.ds(half * cut, size)],
                out_sems.at[half],
            )
        )
        stores[-1].start()
    for store in stores:
        store.wait()


def expand_halves(halves, which, update):
    rows, ranks = halves[0][0].shape
    cut = halves[0][1][0].shape[1]
    counts = tuple(len(pieces) for _, pieces in halves)
    args = [array for columns, pieces in halves for array in (columns, *pieces)]
    return pl.pallas_call(
        functools.partial(expand_kernel, counts=counts, which=which),
        in_specs=[ANYWHERE] * (len(args) + 1),
        out_specs=ANYWHERE,
        out_shape=jax.ShapeDtypeStruct(update.shape, BF16),
        scratch_shapes=[
            pltpu.VMEM((len(halves), rows, ranks), BF16),
            pltpu.VMEM((len(halves), ranks, cut), BF16),
            pltpu.VMEM((len(halves), cut, rows), BF16),
            pltpu.SemaphoreType.DMA((len(halves), max(counts) + 1)),
            pltpu.SemaphoreType.DMA((len(halves),)),
        ],
        input_output_aliases={len(args): 0},
        compiler_params=PARAMS,
        cost_estimate=cost(4 * rows * ranks * cut, 4 * (rows * ranks + ranks * cut + rows * cut)),
    )(*args, update)


def expand_whole_kernel(bases_ref, gathered_ref, out_ref):
    out_ref[0] = (
        jnp.dot(bases_ref[0], gathered_ref[...], preferred_element_type=F32).T.astype(BF16)
    )


def expand_whole(bases, gathered, which, width):
    count, rows, ranks = bases.shape
    tile = gathered.shape[1] // 2
    return pl.pallas_call(
        expand_whole_kernel,
        grid=(gathered.shape[1] // tile,),
        in_specs=[
            pl.BlockSpec((1, rows, ranks), lambda i: (which, 0, 0)),
            pl.BlockSpec((ranks, tile), lambda i: (0, i)),
        ],
        out_specs=pl.BlockSpec((1, tile, rows), lambda i: (which, i, 0)),
        out_shape=jax.ShapeDtypeStruct((count, width, rows), BF16),
        compiler_params=PARAMS,
        cost_estimate=cost(
            2 * rows * ranks * width, 2 * (rows * ranks + ranks * width + rows * width)
        ),
    )(bases, gathered)


def ring_gather(value, first, second):
    row = stack([value] + [receive(value, first, d) for d in (1, 2, 3)])
    half = row.shape[0] // 2
    after = receive(row, second, 1)
    before = receive(row, second, -1)
    far_top = receive(after[:half], second, 1)
    far_bottom = receive(before[half:], second, -1)
    return row, after, far_top, far_bottom, before


def on_device(activations, out_grads, bases, first_moment, second_moment):
    where = jnp.stack([lax.axis_index(n) for n in ("x", "c", "y", "z")]).astype(jnp.int32)
    y, z = where[2], where[3]
    features, ranks = bases.shape[1:]
    part = ranks // (SIDE * SIDE)
    width = first_moment.shape[2]

    other_grads = swap_cores(out_grads)

    column = jnp.arange(ranks)
    slow, fast, inner = column // (SIDE * part), column // part % SIDE, column % part
    source = (((y + slow) % SIDE) * SIDE + (z + fast) % SIDE) * part + inner
    place = (column[:, None] == source[None, :]).astype(BF16)
    own = lax.dynamic_slice_in_dim(activations, (y * SIDE + z) * features, features, 1)
    partial = jnp.einsum("td,kdr->ktr", own, bases, preferred_element_type=F32).astype(BF16)
    partial = jnp.einsum("ktr,rs->kts", partial, place, preferred_element_type=F32).astype(BF16)
    for axis in ("y", "z"):
        size = partial.shape[2] // SIDE
        blocks = [partial[:, :, i * size : (i + 1) * size] for i in range(SIDE)]
        total = blocks[0].astype(F32)
        for i in (1, 3, 2):
            total = total + send(blocks[i], axis, i).astype(F32)
        partial = total.astype(BF16)

    other_partial = swap_cores(partial)
    own_sum, *sums = partial_grads(
        where, partial[0], other_partial[0], out_grads, other_grads, 0, where
    )
    own_sum_1, *sums_1 = partial_grads(
        where, partial[1], other_partial[1], out_grads, other_grads, 1, own_sum
    )
    columns_y, columns_z = arrange(where, bases, 1, own_sum_1)
    sums = [send(value, "x", i + 1) for i, value in enumerate(sums)]
    sums_1 = [send(value, "x", i + 1) for i, value in enumerate(sums_1)]

    *moments, whole = directions(
        own_sum, sums, first_moment, second_moment, 0, 1, [], columns_y
    )
    gathered = lax.all_gather(whole, ("y", "z"), axis=0, tiled=True)

    *moments, left, right = directions(
        own_sum_1, sums_1, first_moment, second_moment, 1, 2, moments, columns_y
    )
    pieces_left = ring_gather(left, "y", "z")
    pieces_right = ring_gather(right, "z", "y")
    update = expand_whole(bases, gathered, 0, width)
    update = expand_halves([(columns_z, pieces_left), (columns_y, pieces_right)], 1, update)
    return jnp.swapaxes(update, 1, 2), *moments


def solution(mesh):
    grid = Mesh(mesh.devices.reshape(4, 2, 4, 4), ("x", "c", "y", "z"))
    dp, fsdp = ("x", "c"), ("y", "z")
    return jax.shard_map(
        on_device,
        mesh=grid,
        in_specs=(
            P(dp, None),
            P(None, dp, None),
            P(None, fsdp, None),
            P(None, fsdp, dp),
            P(None, fsdp, dp),
        ),
        out_specs=(P(None, fsdp, dp), P(None, fsdp, dp), P(None, fsdp, dp)),
        check_vma=False,
    )
```

```python
import functools

import jax
import jax.numpy as jnp
from jax import lax
from jax.experimental import pallas as pl
from jax.experimental.pallas import tpu as pltpu
from jax.sharding import Mesh, PartitionSpec as P

BF16 = jnp.bfloat16
F32 = jnp.float32
SIDE = 4
LANES = 128
VMEM = 56 * 1024 * 1024
PARAMS = pltpu.CompilerParams(vmem_limit_bytes=VMEM)
ANYWHERE = pl.BlockSpec(memory_space=pl.ANY)


def receive(value, axis, distance):
    return lax.ppermute(value, axis, [((i + distance) % SIDE, i) for i in range(SIDE)])


def send(value, axis, distance):
    return receive(value, axis, -distance)


def swap_cores(value):
    return lax.ppermute(value, "c", [(0, 1), (1, 0)])


def held(shape, dtype=BF16):
    return pltpu.HBM(shape, dtype)


def cost(flops, moved):
    return pl.CostEstimate(flops=flops, bytes_accessed=moved, transcendentals=0)


def arrange_kernel(where_ref, bases_ref, _, by_y_ref, by_z_ref):
    y, z = where_ref[2], where_ref[3]
    ranks = bases_ref.shape[2]
    part = ranks // (SIDE * SIDE)
    block = ranks // SIDE
    for out_ref, y_outer in ((by_y_ref, True), (by_z_ref, False)):
        for low in range(0, ranks, block):
            source = lax.broadcasted_iota(jnp.int32, (ranks, block), 0)
            column = lax.broadcasted_iota(jnp.int32, (ranks, block), 1) + low
            outer, inner = column // (SIDE * part), (column // part) & (SIDE - 1)
            dy, dz = (outer, inner) if y_outer else (inner, outer)
            wanted = (((y + dy) & (SIDE - 1)) * SIDE + ((z + dz) & (SIDE - 1))) * part
            wanted = wanted + (column & (part - 1))
            place = jnp.where(source == wanted, 1.0, 0.0).astype(BF16)
            for k in range(bases_ref.shape[0]):
                out_ref[k, :, low : low + block] = jnp.dot(
                    bases_ref[k], place, preferred_element_type=F32
                ).astype(BF16)


def arrange(where, bases, after):
    whole = pl.BlockSpec(bases.shape, lambda i, w: (0, 0, 0))
    return pl.pallas_call(
        arrange_kernel,
        grid_spec=pltpu.PrefetchScalarGridSpec(
            num_scalar_prefetch=1, grid=(1,), in_specs=[whole, ANYWHERE], out_specs=[whole] * 2
        ),
        out_shape=[held(bases.shape)] * 2,
        compiler_params=PARAMS,
        cost_estimate=cost(4 * bases.size * bases.shape[2], 6 * bases.size),
    )(where, bases, after)


def partial_kernel(where_ref, proj_ref, other_proj_ref, grads_ref, other_grads_ref, _, *outs):
    step = pl.program_id(0)
    proj = jnp.concatenate([proj_ref[...], other_proj_ref[...]], axis=0)
    grads = jnp.concatenate([grads_ref[0], other_grads_ref[0]], axis=0)
    total = lax.dot_general(proj, grads, (((0,), (0,)), ((), ())), preferred_element_type=F32)
    span, width = total.shape[1], outs[0].shape[1]
    later = pltpu.roll(total, width, 1)
    total = jnp.where(where_ref[1] == 1, later, total)[:, :width]
    for i, ref in enumerate(outs):

        @pl.when(step == i)
        def _(ref=ref):
            ref[...] = total.astype(ref.dtype)


def partial_grads(where, proj, other_proj, grads, other_grads, which, after):
    tokens, rank_part = proj.shape
    pair = grads.shape[2] // SIDE
    width = pair // 2
    span = (width + LANES - 1) // LANES * LANES
    skip = (pair - span) // LANES

    def window(i, w):
        block = (w[0] + i) & (SIDE - 1)
        return which, 0, pl.multiple_of((block * (pair // LANES) + w[1] * skip) * LANES, LANES)

    small = pl.BlockSpec((tokens, rank_part), lambda i, w: (0, 0))
    large = pl.BlockSpec((pl.Element(1), pl.Element(tokens), pl.Element(span)), window)
    return pl.pallas_call(
        partial_kernel,
        grid_spec=pltpu.PrefetchScalarGridSpec(
            num_scalar_prefetch=1,
            grid=(SIDE,),
            in_specs=[small, small, large, large, ANYWHERE],
            out_specs=[pl.BlockSpec((rank_part, width), lambda i, w: (0, 0))] * SIDE,
        ),
        out_shape=[held((rank_part, width), F32)] + [held((rank_part, width))] * (SIDE - 1),
        compiler_params=PARAMS,
        cost_estimate=cost(
            4 * tokens * rank_part * width * SIDE, 4 * (tokens + rank_part) * width * SIDE
        ),
    )(where, proj, other_proj, grads, other_grads, after)


def direction_kernel(*refs, pieces):
    own_ref, first_ref, second_ref = refs[0], refs[4], refs[5]
    new_first_ref, new_second_ref = refs[-2 - pieces : -pieces]
    gradient = own_ref[...]
    for ref in refs[1:4]:
        gradient = gradient + ref[...].astype(F32)
    new_first = 0.9 * first_ref[0] + 0.1 * gradient
    new_second = 0.999 * second_ref[0] + 0.001 * gradient * gradient
    new_first_ref[0] = new_first
    new_second_ref[0] = new_second
    first_fix = 1.0 - 0.9**1000.0
    second_fix = 1.0 - 0.999**1000.0
    root = jnp.sqrt(new_second * (1.0 / second_fix)) + 1e-08
    direction = (new_first * (1.0 / first_fix) / root).astype(BF16)
    low = 0
    for ref in refs[-pieces:]:
        size = min(ref.shape[1], direction.shape[1] - low)
        ref[:, :size] = direction[:, low : low + size]
        if size < ref.shape[1]:
            ref[:, size:] = jnp.zeros((ref.shape[0], ref.shape[1] - size), BF16)
        low += size


def directions(own_sum, sums, first_moment, second_moment, which, pieces, before, after):
    _, rows, width = first_moment.shape
    cut = (width // pieces + LANES - 1) // LANES * LANES
    tile = 32
    flat = pl.BlockSpec((tile, width), lambda i: (i, 0))
    own = pl.BlockSpec((1, tile, width), lambda i: (which, i, 0))
    half = pl.BlockSpec((tile, cut), lambda i: (i, 0))
    in_specs = [flat] * SIDE + [own, own]
    args = [own_sum, *sums, first_moment, second_moment]
    aliases = {len(args) + i: i for i in range(len(before))}
    args += [*before, after]
    in_specs += [ANYWHERE] * (len(before) + 1)
    piece = held((rows, cut))
    full = jax.ShapeDtypeStruct(first_moment.shape, F32)
    return pl.pallas_call(
        functools.partial(direction_kernel, pieces=pieces),
        grid=(rows // tile,),
        in_specs=in_specs,
        out_specs=[own, own] + [half] * pieces,
        out_shape=[full, full] + [piece] * pieces,
        input_output_aliases=aliases,
        compiler_params=PARAMS,
        cost_estimate=cost(30 * rows * width, 26 * rows * width),
    )(*args)


def stack_kernel(*refs):
    rows = refs[0].shape[0]
    for i, ref in enumerate(refs[:-1]):
        refs[-1][i * rows : (i + 1) * rows, :] = ref[...]


def stack(pieces):
    rows, width = pieces[0].shape
    return pl.pallas_call(
        stack_kernel,
        out_shape=held((rows * len(pieces), width)),
        compiler_params=PARAMS,
        cost_estimate=cost(0, 4 * rows * width * len(pieces)),
    )(*pieces)


def expand_kernel(*refs, counts, which):
    halves = len(counts)
    out_ref, columns, pieces, outs, in_sems, out_sems = refs[-6:]
    cut = pieces.shape[2]
    loads, refs = [], list(refs)
    for half, count in enumerate(counts):
        loads.append([(refs.pop(0).at[which], columns.at[half])])
        at = 0
        for _ in range(count):
            ref = refs.pop(0)
            loads[half].append((ref, pieces.at[half, pl.ds(at, ref.shape[0])]))
            at += ref.shape[0]
    copies = [
        [pltpu.make_async_copy(a, b, in_sems.at[half, i]) for i, (a, b) in enumerate(group)]
        for half, group in enumerate(loads)
    ]
    for group in copies:
        for copy in group:
            copy.start()
    stores = []
    for half, group in enumerate(copies):
        for copy in group:
            copy.wait()
        for low in range(0, cut, 256):
            high = min(low + 256, cut)
            total = jnp.dot(columns[half], pieces[half, :, low:high], preferred_element_type=F32)
            outs[half, low:high, :] = total.T.astype(BF16)
        size = min(cut, out_ref.shape[1] - half * cut)
        stores.append(
            pltpu.make_async_copy(
                outs.at[half, pl.ds(0, size)],
                out_ref.at[which, pl.ds(half * cut, size)],
                out_sems.at[half],
            )
        )
        stores[-1].start()
    for store in stores:
        store.wait()


def expand_halves(halves, which, width, update):
    count, rows, ranks = halves[0][0].shape
    cut = halves[0][1][0].shape[1]
    counts = tuple(len(pieces) for _, pieces in halves)
    args = [array for columns, pieces in halves for array in (columns, *pieces)]
    aliases = {}
    if update is not None:
        aliases = {len(args): 0}
        args.append(update)
    return pl.pallas_call(
        functools.partial(expand_kernel, counts=counts, which=which),
        in_specs=[ANYWHERE] * len(args),
        out_specs=ANYWHERE,
        out_shape=jax.ShapeDtypeStruct((count, width, rows), BF16),
        scratch_shapes=[
            pltpu.VMEM((len(halves), rows, ranks), BF16),
            pltpu.VMEM((len(halves), ranks, cut), BF16),
            pltpu.VMEM((len(halves), cut, rows), BF16),
            pltpu.SemaphoreType.DMA((len(halves), max(counts) + 1)),
            pltpu.SemaphoreType.DMA((len(halves),)),
        ],
        input_output_aliases=aliases,
        compiler_params=PARAMS,
        cost_estimate=cost(4 * rows * ranks * cut, 4 * (rows * ranks + ranks * cut + rows * cut)),
    )(*args)


def ring_gather(value, first, second, split):
    row = stack([value] + [receive(value, first, d) for d in (1, 2, 3)])
    after = receive(row, second, 1)
    before = receive(row, second, -1)
    if not split:
        return row, after, receive(after, second, 1), before
    half = row.shape[0] // 2
    far_top = receive(after[:half], second, 1)
    far_bottom = receive(before[half:], second, -1)
    return row, after, far_top, far_bottom, before


def on_device(activations, out_grads, bases, first_moment, second_moment):
    where = jnp.stack([lax.axis_index(n) for n in ("x", "c", "y", "z")]).astype(jnp.int32)
    y, z = where[2], where[3]
    features, ranks = bases.shape[1:]
    part = ranks // (SIDE * SIDE)
    width = first_moment.shape[2]

    other_grads = swap_cores(out_grads)

    column = jnp.arange(ranks)
    slow, fast, inner = column // (SIDE * part), column // part % SIDE, column % part
    source = (((y + slow) % SIDE) * SIDE + (z + fast) % SIDE) * part + inner
    place = (column[:, None] == source[None, :]).astype(BF16)
    own = lax.dynamic_slice_in_dim(activations, (y * SIDE + z) * features, features, 1)
    partial = jnp.einsum("td,kdr->ktr", own, bases, preferred_element_type=F32).astype(BF16)
    partial = jnp.einsum("ktr,rs->kts", partial, place, preferred_element_type=F32).astype(BF16)
    for axis in ("y", "z"):
        size = partial.shape[2] // SIDE
        blocks = [partial[:, :, i * size : (i + 1) * size] for i in range(SIDE)]
        total = blocks[0].astype(F32)
        for i in (1, 3, 2):
            total = total + send(blocks[i], axis, i).astype(F32)
        partial = total.astype(BF16)

    other_partial = swap_cores(partial)
    own_sum, *sums = partial_grads(
        where, partial[0], other_partial[0], out_grads, other_grads, 0, where
    )
    own_sum_1, *sums_1 = partial_grads(
        where, partial[1], other_partial[1], out_grads, other_grads, 1, own_sum
    )
    columns_y, columns_z = arrange(where, bases, own_sum_1)
    sums = [send(value, "x", i + 1) for i, value in enumerate(sums)]
    sums_1 = [send(value, "x", i + 1) for i, value in enumerate(sums_1)]

    moments, update = [], None
    for which, parts in enumerate(([own_sum, sums], [own_sum_1, sums_1])):
        *moments, left, right = directions(
            *parts, first_moment, second_moment, which, 2, moments, columns_y
        )
        halves = [
            (columns_z, ring_gather(left, "y", "z", which == 1)),
            (columns_y, ring_gather(right, "z", "y", which == 1)),
        ]
        update = expand_halves(halves, which, width, update)
    return jnp.swapaxes(update, 1, 2), *moments


def solution(mesh):
    grid = Mesh(mesh.devices.reshape(4, 2, 4, 4), ("x", "c", "y", "z"))
    dp, fsdp = ("x", "c"), ("y", "z")
    return jax.shard_map(
        on_device,
        mesh=grid,
        in_specs=(
            P(dp, None),
            P(None, dp, None),
            P(None, fsdp, None),
            P(None, fsdp, dp),
            P(None, fsdp, dp),
        ),
        out_specs=(P(None, fsdp, dp), P(None, fsdp, dp), P(None, fsdp, dp)),
        check_vma=False,
    )
```

```python
import functools

import jax
import jax.numpy as jnp
from jax import lax
from jax.experimental import pallas as pl
from jax.experimental.pallas import tpu as pltpu
from jax.sharding import Mesh, PartitionSpec as P

BF16 = jnp.bfloat16
F32 = jnp.float32
SIDE = 4
LANES = 128
VMEM = 56 * 1024 * 1024
PARAMS = pltpu.CompilerParams(vmem_limit_bytes=VMEM)
ANYWHERE = pl.BlockSpec(memory_space=pl.ANY)


def receive(value, axis, distance):
    return lax.ppermute(value, axis, [((i + distance) % SIDE, i) for i in range(SIDE)])


def send(value, axis, distance):
    return receive(value, axis, -distance)


def swap_cores(value):
    return lax.ppermute(value, "c", [(0, 1), (1, 0)])


def held(shape, dtype=BF16):
    return pltpu.HBM(shape, dtype)


def cost(flops, moved):
    return pl.CostEstimate(flops=flops, bytes_accessed=moved, transcendentals=0)


def arrange_kernel(where_ref, bases_ref, _, by_y_ref, by_z_ref):
    y, z = where_ref[2], where_ref[3]
    ranks = bases_ref.shape[2]
    part = ranks // (SIDE * SIDE)
    block = ranks // SIDE
    for out_ref, y_outer in ((by_y_ref, True), (by_z_ref, False)):
        for low in range(0, ranks, block):
            source = lax.broadcasted_iota(jnp.int32, (ranks, block), 0)
            column = lax.broadcasted_iota(jnp.int32, (ranks, block), 1) + low
            outer, inner = column // (SIDE * part), (column // part) & (SIDE - 1)
            dy, dz = (outer, inner) if y_outer else (inner, outer)
            wanted = (((y + dy) & (SIDE - 1)) * SIDE + ((z + dz) & (SIDE - 1))) * part
            wanted = wanted + (column & (part - 1))
            place = jnp.where(source == wanted, 1.0, 0.0).astype(BF16)
            for k in range(bases_ref.shape[0]):
                out_ref[k, :, low : low + block] = jnp.dot(
                    bases_ref[k], place, preferred_element_type=F32
                ).astype(BF16)


def arrange(where, bases, after):
    whole = pl.BlockSpec(bases.shape, lambda i, w: (0, 0, 0))
    return pl.pallas_call(
        arrange_kernel,
        grid_spec=pltpu.PrefetchScalarGridSpec(
            num_scalar_prefetch=1, grid=(1,), in_specs=[whole, ANYWHERE], out_specs=[whole] * 2
        ),
        out_shape=[held(bases.shape)] * 2,
        compiler_params=PARAMS,
        cost_estimate=cost(4 * bases.size * bases.shape[2], 6 * bases.size),
    )(where, bases, after)


def partial_kernel(where_ref, proj_ref, other_proj_ref, grads_ref, other_grads_ref, _, *outs):
    step = pl.program_id(0)
    proj = jnp.concatenate([proj_ref[...], other_proj_ref[...]], axis=0)
    grads = jnp.concatenate([grads_ref[0], other_grads_ref[0]], axis=0)
    total = lax.dot_general(proj, grads, (((0,), (0,)), ((), ())), preferred_element_type=F32)
    span, width = total.shape[1], outs[0].shape[1]
    later = pltpu.roll(total, width, 1)
    total = jnp.where(where_ref[1] == 1, later, total)[:, :width]
    for i, ref in enumerate(outs):

        @pl.when(step == i)
        def _(ref=ref):
            ref[...] = total.astype(ref.dtype)


def partial_grads(where, proj, other_proj, grads, other_grads, which, after):
    tokens, rank_part = proj.shape
    pair = grads.shape[2] // SIDE
    width = pair // 2
    span = (width + LANES - 1) // LANES * LANES
    skip = (pair - span) // LANES

    def window(i, w):
        block = (w[0] + i) & (SIDE - 1)
        return which, 0, pl.multiple_of((block * (pair // LANES) + w[1] * skip) * LANES, LANES)

    small = pl.BlockSpec((tokens, rank_part), lambda i, w: (0, 0))
    large = pl.BlockSpec((pl.Element(1), pl.Element(tokens), pl.Element(span)), window)
    return pl.pallas_call(
        partial_kernel,
        grid_spec=pltpu.PrefetchScalarGridSpec(
            num_scalar_prefetch=1,
            grid=(SIDE,),
            in_specs=[small, small, large, large, ANYWHERE],
            out_specs=[pl.BlockSpec((rank_part, width), lambda i, w: (0, 0))] * SIDE,
        ),
        out_shape=[held((rank_part, width), F32)] + [held((rank_part, width))] * (SIDE - 1),
        compiler_params=PARAMS,
        cost_estimate=cost(
            4 * tokens * rank_part * width * SIDE, 4 * (tokens + rank_part) * width * SIDE
        ),
    )(where, proj, other_proj, grads, other_grads, after)


def direction_kernel(*refs, pieces):
    own_ref, first_ref, second_ref = refs[0], refs[4], refs[5]
    new_first_ref, new_second_ref = refs[-2 - pieces : -pieces]
    gradient = own_ref[...]
    for ref in refs[1:4]:
        gradient = gradient + ref[...].astype(F32)
    new_first = 0.9 * first_ref[0] + 0.1 * gradient
    new_second = 0.999 * second_ref[0] + 0.001 * gradient * gradient
    new_first_ref[0] = new_first
    new_second_ref[0] = new_second
    first_fix = 1.0 - 0.9**1000.0
    second_fix = 1.0 - 0.999**1000.0
    root = jnp.sqrt(new_second * (1.0 / second_fix)) + 1e-08
    direction = (new_first * (1.0 / first_fix) / root).astype(BF16)
    low = 0
    for ref in refs[-pieces:]:
        size = min(ref.shape[1], direction.shape[1] - low)
        ref[:, :size] = direction[:, low : low + size]
        if size < ref.shape[1]:
            ref[:, size:] = jnp.zeros((ref.shape[0], ref.shape[1] - size), BF16)
        low += size


def directions(own_sum, sums, first_moment, second_moment, which, pieces, before, after):
    _, rows, width = first_moment.shape
    cut = (width // pieces + LANES - 1) // LANES * LANES
    tile = 32
    flat = pl.BlockSpec((tile, width), lambda i: (i, 0))
    own = pl.BlockSpec((1, tile, width), lambda i: (which, i, 0))
    half = pl.BlockSpec((tile, cut), lambda i: (i, 0))
    in_specs = [flat] * SIDE + [own, own]
    args = [own_sum, *sums, first_moment, second_moment]
    aliases = {len(args) + i: i for i in range(len(before))}
    args += [*before, after]
    in_specs += [ANYWHERE] * (len(before) + 1)
    piece = held((rows, cut))
    full = jax.ShapeDtypeStruct(first_moment.shape, F32)
    return pl.pallas_call(
        functools.partial(direction_kernel, pieces=pieces),
        grid=(rows // tile,),
        in_specs=in_specs,
        out_specs=[own, own] + [half] * pieces,
        out_shape=[full, full] + [piece] * pieces,
        input_output_aliases=aliases,
        compiler_params=PARAMS,
        cost_estimate=cost(30 * rows * width, 26 * rows * width),
    )(*args)


def stack_kernel(*refs):
    rows = refs[0].shape[0]
    for i, ref in enumerate(refs[:-1]):
        refs[-1][i * rows : (i + 1) * rows, :] = ref[...]


def stack(pieces):
    rows, width = pieces[0].shape
    return pl.pallas_call(
        stack_kernel,
        out_shape=held((rows * len(pieces), width)),
        compiler_params=PARAMS,
        cost_estimate=cost(0, 4 * rows * width * len(pieces)),
    )(*pieces)


def expand_kernel(*refs, counts, which):
    halves = len(counts)
    out_ref, columns, pieces, outs, in_sems, out_sems = refs[-6:]
    cut = pieces.shape[2]
    loads, refs = [], list(refs)
    for half, count in enumerate(counts):
        loads.append([(refs.pop(0).at[which], columns.at[half])])
        at = 0
        for _ in range(count):
            ref = refs.pop(0)
            loads[half].append((ref, pieces.at[half, pl.ds(at, ref.shape[0])]))
            at += ref.shape[0]
    copies = [
        [pltpu.make_async_copy(a, b, in_sems.at[half, i]) for i, (a, b) in enumerate(group)]
        for half, group in enumerate(loads)
    ]
    for group in copies:
        for copy in group:
            copy.start()
    stores = []
    for half, group in enumerate(copies):
        for copy in group:
            copy.wait()
        for low in range(0, cut, 256):
            high = min(low + 256, cut)
            total = jnp.dot(columns[half], pieces[half, :, low:high], preferred_element_type=F32)
            outs[half, low:high, :] = total.T.astype(BF16)
        size = min(cut, out_ref.shape[1] - half * cut)
        stores.append(
            pltpu.make_async_copy(
                outs.at[half, pl.ds(0, size)],
                out_ref.at[which, pl.ds(half * cut, size)],
                out_sems.at[half],
            )
        )
        stores[-1].start()
    for store in stores:
        store.wait()


def expand_halves(halves, which, width, update):
    count, rows, ranks = halves[0][0].shape
    cut = halves[0][1][0].shape[1]
    counts = tuple(len(pieces) for _, pieces in halves)
    args = [array for columns, pieces in halves for array in (columns, *pieces)]
    aliases = {}
    if update is not None:
        aliases = {len(args): 0}
        args.append(update)
    return pl.pallas_call(
        functools.partial(expand_kernel, counts=counts, which=which),
        in_specs=[ANYWHERE] * len(args),
        out_specs=ANYWHERE,
        out_shape=jax.ShapeDtypeStruct((count, width, rows), BF16),
        scratch_shapes=[
            pltpu.VMEM((len(halves), rows, ranks), BF16),
            pltpu.VMEM((len(halves), ranks, cut), BF16),
            pltpu.VMEM((len(halves), cut, rows), BF16),
            pltpu.SemaphoreType.DMA((len(halves), max(counts) + 1)),
            pltpu.SemaphoreType.DMA((len(halves),)),
        ],
        input_output_aliases=aliases,
        compiler_params=PARAMS,
        cost_estimate=cost(4 * rows * ranks * cut, 4 * (rows * ranks + ranks * cut + rows * cut)),
    )(*args)


def ring_gather(value, first, second, split):
    row = stack([value] + [receive(value, first, d) for d in (1, 2, 3)])
    after = receive(row, second, 1)
    before = receive(row, second, -1)
    if not split:
        return row, after, receive(after, second, 1), before
    half = row.shape[0] // 2
    far_top = receive(after[:half], second, 1)
    far_bottom = receive(before[half:], second, -1)
    return row, after, far_top, far_bottom, before


def on_device(activations, out_grads, bases, first_moment, second_moment):
    where = jnp.stack([lax.axis_index(n) for n in ("x", "c", "y", "z")]).astype(jnp.int32)
    y, z = where[2], where[3]
    features, ranks = bases.shape[1:]
    part = ranks // (SIDE * SIDE)
    width = first_moment.shape[2]

    other_grads = swap_cores(out_grads)

    column = jnp.arange(ranks)
    slow, fast, inner = column // (SIDE * part), column // part % SIDE, column % part
    source = (((y + slow) % SIDE) * SIDE + (z + fast) % SIDE) * part + inner
    place = (column[:, None] == source[None, :]).astype(BF16)
    own = lax.dynamic_slice_in_dim(activations, (y * SIDE + z) * features, features, 1)
    partial = jnp.einsum("td,kdr->ktr", own, bases, preferred_element_type=F32).astype(BF16)
    partial = jnp.einsum("ktr,rs->kts", partial, place, preferred_element_type=F32).astype(BF16)
    for axis in ("y", "z"):
        size = partial.shape[2] // SIDE
        blocks = [partial[:, :, i * size : (i + 1) * size] for i in range(SIDE)]
        total = blocks[0].astype(F32)
        for i in (1, 3, 2):
            total = total + send(blocks[i], axis, i).astype(F32)
        partial = total.astype(BF16)

    other_partial = swap_cores(partial)
    own_sum, *sums = partial_grads(
        where, partial[0], other_partial[0], out_grads, other_grads, 0, where
    )
    own_sum_1, *sums_1 = partial_grads(
        where, partial[1], other_partial[1], out_grads, other_grads, 1, own_sum
    )
    columns_y, columns_z = arrange(where, bases, own_sum_1)
    sums = [send(value, "x", i + 1) for i, value in enumerate(sums)]
    sums_1 = [send(value, "x", i + 1) for i, value in enumerate(sums_1)]

    moments, update, after = [], None, columns_y
    for which, parts in enumerate(([own_sum, sums], [own_sum_1, sums_1])):
        *moments, left, right = directions(
            *parts, first_moment, second_moment, which, 2, moments, after
        )
        halves = [
            (columns_z, ring_gather(left, "y", "z", which == 1)),
            (columns_y, ring_gather(right, "z", "y", which == 1)),
        ]
        after = halves[0][1][0]
        update = expand_halves(halves, which, width, update)
    return jnp.swapaxes(update, 1, 2), *moments


def solution(mesh):
    grid = Mesh(mesh.devices.reshape(4, 2, 4, 4), ("x", "c", "y", "z"))
    dp, fsdp = ("x", "c"), ("y", "z")
    return jax.shard_map(
        on_device,
        mesh=grid,
        in_specs=(
            P(dp, None),
            P(None, dp, None),
            P(None, fsdp, None),
            P(None, fsdp, dp),
            P(None, fsdp, dp),
        ),
        out_specs=(P(None, fsdp, dp), P(None, fsdp, dp), P(None, fsdp, dp)),
        check_vma=False,
    )
```

```python
import functools

import jax
import jax.numpy as jnp
from jax import lax
from jax.experimental import pallas as pl
from jax.experimental.pallas import tpu as pltpu
from jax.sharding import Mesh, PartitionSpec as P

BF16 = jnp.bfloat16
F32 = jnp.float32
SIDE = 4
LANES = 128
VMEM = 56 * 1024 * 1024
PARAMS = pltpu.CompilerParams(vmem_limit_bytes=VMEM)
ANYWHERE = pl.BlockSpec(memory_space=pl.ANY)


def receive(value, axis, distance):
    return lax.ppermute(value, axis, [((i + distance) % SIDE, i) for i in range(SIDE)])


def send(value, axis, distance):
    return receive(value, axis, -distance)


def swap_cores(value):
    return lax.ppermute(value, "c", [(0, 1), (1, 0)])


def held(shape, dtype=BF16):
    return pltpu.HBM(shape, dtype)


def cost(flops, moved):
    return pl.CostEstimate(flops=flops, bytes_accessed=moved, transcendentals=0)


def arrange_kernel(where_ref, bases_ref, _, by_y_ref, by_z_ref):
    y, z = where_ref[2], where_ref[3]
    ranks = bases_ref.shape[2]
    part = ranks // (SIDE * SIDE)
    block = ranks // SIDE
    for out_ref, y_outer in ((by_y_ref, True), (by_z_ref, False)):
        for low in range(0, ranks, block):
            source = lax.broadcasted_iota(jnp.int32, (ranks, block), 0)
            column = lax.broadcasted_iota(jnp.int32, (ranks, block), 1) + low
            outer, inner = column // (SIDE * part), (column // part) & (SIDE - 1)
            dy, dz = (outer, inner) if y_outer else (inner, outer)
            wanted = (((y + dy) & (SIDE - 1)) * SIDE + ((z + dz) & (SIDE - 1))) * part
            wanted = wanted + (column & (part - 1))
            place = jnp.where(source == wanted, 1.0, 0.0).astype(BF16)
            for k in range(bases_ref.shape[0]):
                out_ref[k, :, low : low + block] = jnp.dot(
                    bases_ref[k], place, preferred_element_type=F32
                ).astype(BF16)


def arrange(where, bases, after):
    whole = pl.BlockSpec(bases.shape, lambda i, w: (0, 0, 0))
    return pl.pallas_call(
        arrange_kernel,
        grid_spec=pltpu.PrefetchScalarGridSpec(
            num_scalar_prefetch=1, grid=(1,), in_specs=[whole, ANYWHERE], out_specs=[whole] * 2
        ),
        out_shape=[held(bases.shape)] * 2,
        compiler_params=PARAMS,
        cost_estimate=cost(4 * bases.size * bases.shape[2], 6 * bases.size),
    )(where, bases, after)


def partial_kernel(where_ref, proj_ref, other_proj_ref, grads_ref, other_grads_ref, _, *outs):
    step = pl.program_id(0)
    proj = jnp.concatenate([proj_ref[0], other_proj_ref[0]], axis=0)
    grads = jnp.concatenate([grads_ref[0], other_grads_ref[0]], axis=0)
    total = lax.dot_general(proj, grads, (((0,), (0,)), ((), ())), preferred_element_type=F32)
    span, width = total.shape[1], outs[0].shape[1]
    later = pltpu.roll(total, width, 1)
    total = jnp.where(where_ref[1] == 1, later, total)[:, :width]
    for i, ref in enumerate(outs):

        @pl.when(step == i)
        def _(ref=ref):
            ref[...] = total.astype(ref.dtype)


def partial_grads(where, proj, other_proj, grads, other_grads, which, after):
    _, tokens, rank_part = proj.shape
    pair = grads.shape[2] // SIDE
    width = pair // 2
    span = (width + LANES - 1) // LANES * LANES
    skip = (pair - span) // LANES

    def window(i, w):
        block = (w[0] + i) & (SIDE - 1)
        return which, 0, pl.multiple_of((block * (pair // LANES) + w[1] * skip) * LANES, LANES)

    small = pl.BlockSpec((1, tokens, rank_part), lambda i, w: (which, 0, 0))
    large = pl.BlockSpec((pl.Element(1), pl.Element(tokens), pl.Element(span)), window)
    return pl.pallas_call(
        partial_kernel,
        grid_spec=pltpu.PrefetchScalarGridSpec(
            num_scalar_prefetch=1,
            grid=(SIDE,),
            in_specs=[small, small, large, large, ANYWHERE],
            out_specs=[pl.BlockSpec((rank_part, width), lambda i, w: (0, 0))] * SIDE,
        ),
        out_shape=[held((rank_part, width), F32)] + [held((rank_part, width))] * (SIDE - 1),
        compiler_params=PARAMS,
        cost_estimate=cost(
            4 * tokens * rank_part * width * SIDE, 4 * (tokens + rank_part) * width * SIDE
        ),
    )(where, proj, other_proj, grads, other_grads, after)


def direction_kernel(*refs, pieces):
    own_ref, first_ref, second_ref = refs[0], refs[4], refs[5]
    new_first_ref, new_second_ref = refs[-2 - pieces : -pieces]
    gradient = own_ref[...]
    for ref in refs[1:4]:
        gradient = gradient + ref[...].astype(F32)
    new_first = 0.9 * first_ref[0] + 0.1 * gradient
    new_second = 0.999 * second_ref[0] + 0.001 * gradient * gradient
    new_first_ref[0] = new_first
    new_second_ref[0] = new_second
    first_fix = 1.0 - 0.9**1000.0
    second_fix = 1.0 - 0.999**1000.0
    root = jnp.sqrt(new_second * (1.0 / second_fix)) + 1e-08
    direction = (new_first * (1.0 / first_fix) / root).astype(BF16)
    low = 0
    for ref in refs[-pieces:]:
        size = min(ref.shape[1], direction.shape[1] - low)
        ref[:, :size] = direction[:, low : low + size]
        if size < ref.shape[1]:
            ref[:, size:] = jnp.zeros((ref.shape[0], ref.shape[1] - size), BF16)
        low += size


def directions(own_sum, sums, first_moment, second_moment, which, pieces, before, after):
    _, rows, width = first_moment.shape
    cut = (width // pieces + LANES - 1) // LANES * LANES
    tile = 32
    flat = pl.BlockSpec((tile, width), lambda i: (i, 0))
    own = pl.BlockSpec((1, tile, width), lambda i: (which, i, 0))
    half = pl.BlockSpec((tile, cut), lambda i: (i, 0))
    in_specs = [flat] * SIDE + [own, own]
    args = [own_sum, *sums, first_moment, second_moment]
    aliases = {len(args) + i: i for i in range(len(before))}
    args += [*before, after]
    in_specs += [ANYWHERE] * (len(before) + 1)
    piece = held((rows, cut))
    full = jax.ShapeDtypeStruct(first_moment.shape, F32)
    return pl.pallas_call(
        functools.partial(direction_kernel, pieces=pieces),
        grid=(rows // tile,),
        in_specs=in_specs,
        out_specs=[own, own] + [half] * pieces,
        out_shape=[full, full] + [piece] * pieces,
        input_output_aliases=aliases,
        compiler_params=PARAMS,
        cost_estimate=cost(30 * rows * width, 26 * rows * width),
    )(*args)


def stack_kernel(*refs):
    rows = refs[0].shape[0]
    for i, ref in enumerate(refs[:-1]):
        refs[-1][i * rows : (i + 1) * rows, :] = ref[...]


def stack(pieces):
    rows, width = pieces[0].shape
    return pl.pallas_call(
        stack_kernel,
        out_shape=held((rows * len(pieces), width)),
        compiler_params=PARAMS,
        cost_estimate=cost(0, 4 * rows * width * len(pieces)),
    )(*pieces)


def expand_kernel(*refs, counts, which):
    halves = len(counts)
    out_ref, columns, pieces, outs, in_sems, out_sems = refs[-6:]
    cut = pieces.shape[2]
    loads, refs = [], list(refs)
    for half, count in enumerate(counts):
        loads.append([(refs.pop(0).at[which], columns.at[half])])
        at = 0
        for _ in range(count):
            ref = refs.pop(0)
            loads[half].append((ref, pieces.at[half, pl.ds(at, ref.shape[0])]))
            at += ref.shape[0]
    copies = [
        [pltpu.make_async_copy(a, b, in_sems.at[half, i]) for i, (a, b) in enumerate(group)]
        for half, group in enumerate(loads)
    ]
    for group in copies:
        for copy in group:
            copy.start()
    stores = []
    for half, group in enumerate(copies):
        for copy in group:
            copy.wait()
        outs[half] = lax.dot_general(
            pieces[half], columns[half], (((0,), (1,)), ((), ())), preferred_element_type=F32
        ).astype(BF16)
        size = min(cut, out_ref.shape[1] - half * cut)
        stores.append(
            pltpu.make_async_copy(
                outs.at[half, pl.ds(0, size)],
                out_ref.at[which, pl.ds(half * cut, size)],
                out_sems.at[half],
            )
        )
        stores[-1].start()
    for store in stores:
        store.wait()


def expand_halves(halves, which, width, update):
    count, rows, ranks = halves[0][0].shape
    cut = halves[0][1][0].shape[1]
    counts = tuple(len(pieces) for _, pieces in halves)
    args = [array for columns, pieces in halves for array in (columns, *pieces)]
    aliases = {}
    if update is not None:
        aliases = {len(args): 0}
        args.append(update)
    return pl.pallas_call(
        functools.partial(expand_kernel, counts=counts, which=which),
        in_specs=[ANYWHERE] * len(args),
        out_specs=ANYWHERE,
        out_shape=jax.ShapeDtypeStruct((count, width, rows), BF16),
        scratch_shapes=[
            pltpu.VMEM((len(halves), rows, ranks), BF16),
            pltpu.VMEM((len(halves), ranks, cut), BF16),
            pltpu.VMEM((len(halves), cut, rows), BF16),
            pltpu.SemaphoreType.DMA((len(halves), max(counts) + 1)),
            pltpu.SemaphoreType.DMA((len(halves),)),
        ],
        input_output_aliases=aliases,
        compiler_params=PARAMS,
        cost_estimate=cost(4 * rows * ranks * cut, 4 * (rows * ranks + ranks * cut + rows * cut)),
    )(*args)


def ring_gather(value, first, second, split):
    row = stack([value] + [receive(value, first, d) for d in (1, 2, 3)])
    after = receive(row, second, 1)
    before = receive(row, second, -1)
    if not split:
        return row, after, receive(after, second, 1), before
    half = row.shape[0] // 2
    far_top = receive(after[:half], second, 1)
    far_bottom = receive(before[half:], second, -1)
    return row, after, far_top, far_bottom, before


def on_device(activations, out_grads, bases, first_moment, second_moment):
    where = jnp.stack([lax.axis_index(n) for n in ("x", "c", "y", "z")]).astype(jnp.int32)
    y, z = where[2], where[3]
    features, ranks = bases.shape[1:]
    part = ranks // (SIDE * SIDE)
    width = first_moment.shape[2]

    other_grads = swap_cores(out_grads)

    column = jnp.arange(ranks)
    slow, fast, inner = column // (SIDE * part), column // part % SIDE, column % part
    source = (((y + slow) % SIDE) * SIDE + (z + fast) % SIDE) * part + inner
    place = (column[:, None] == source[None, :]).astype(BF16)
    own = lax.dynamic_slice_in_dim(activations, (y * SIDE + z) * features, features, 1)
    partial = jnp.einsum("td,kdr->ktr", own, bases, preferred_element_type=F32).astype(BF16)
    partial = jnp.einsum("ktr,rs->kts", partial, place, preferred_element_type=F32).astype(BF16)
    for axis in ("y", "z"):
        size = partial.shape[2] // SIDE
        blocks = [partial[:, :, i * size : (i + 1) * size] for i in range(SIDE)]
        total = blocks[0].astype(F32)
        for i in (1, 3, 2):
            total = total + send(blocks[i], axis, i).astype(F32)
        partial = total.astype(BF16)

    other_partial = swap_cores(partial)
    own_sum, *sums = partial_grads(
        where, partial, other_partial, out_grads, other_grads, 0, where
    )
    own_sum_1, *sums_1 = partial_grads(
        where, partial, other_partial, out_grads, other_grads, 1, own_sum
    )
    columns_y, columns_z = arrange(where, bases, own_sum_1)
    sums = [send(value, "x", i + 1) for i, value in enumerate(sums)]
    sums_1 = [send(value, "x", i + 1) for i, value in enumerate(sums_1)]

    moments, update, after = [], None, columns_y
    for which, parts in enumerate(([own_sum, sums], [own_sum_1, sums_1])):
        *moments, left, right = directions(
            *parts, first_moment, second_moment, which, 2, moments, after
        )
        halves = [
            (columns_z, ring_gather(left, "y", "z", which == 1)),
            (columns_y, ring_gather(right, "z", "y", which == 1)),
        ]
        after = halves[0][1][0]
        update = expand_halves(halves, which, width, update)
    return jnp.swapaxes(update, 1, 2), *moments


def solution(mesh):
    grid = Mesh(mesh.devices.reshape(4, 2, 4, 4), ("x", "c", "y", "z"))
    dp, fsdp = ("x", "c"), ("y", "z")
    return jax.shard_map(
        on_device,
        mesh=grid,
        in_specs=(
            P(dp, None),
            P(None, dp, None),
            P(None, fsdp, None),
            P(None, fsdp, dp),
            P(None, fsdp, dp),
        ),
        out_specs=(P(None, fsdp, dp), P(None, fsdp, dp), P(None, fsdp, dp)),
        check_vma=False,
    )
```

```python
import functools

import jax
import jax.numpy as jnp
from jax import lax
from jax.experimental import pallas as pl
from jax.experimental.pallas import tpu as pltpu
from jax.sharding import Mesh, PartitionSpec as P

BF16 = jnp.bfloat16
F32 = jnp.float32
SIDE = 4
LANES = 128
VMEM = 56 * 1024 * 1024
PARAMS = pltpu.CompilerParams(vmem_limit_bytes=VMEM)
ANYWHERE = pl.BlockSpec(memory_space=pl.ANY)


def receive(value, axis, distance):
    return lax.ppermute(value, axis, [((i + distance) % SIDE, i) for i in range(SIDE)])


def send(value, axis, distance):
    return receive(value, axis, -distance)


def swap_cores(value):
    return lax.ppermute(value, "c", [(0, 1), (1, 0)])


def held(shape, dtype=BF16):
    return pltpu.HBM(shape, dtype)


def cost(flops, moved):
    return pl.CostEstimate(flops=flops, bytes_accessed=moved, transcendentals=0)


def arrange_kernel(where_ref, bases_ref, _, by_y_ref, by_z_ref):
    y, z = where_ref[2], where_ref[3]
    ranks = bases_ref.shape[2]
    part = ranks // (SIDE * SIDE)
    block = ranks // SIDE
    source = lax.broadcasted_iota(jnp.int32, (block, block), 0)
    column = lax.broadcasted_iota(jnp.int32, (block, block), 1)
    wanted = ((z + column // part) & (SIDE - 1)) * part + (column & (part - 1))
    place = jnp.where(source == wanted, 1.0, 0.0).astype(BF16)
    for dy in range(SIDE):
        start = pl.multiple_of(((y + dy) & (SIDE - 1)) * block, block)
        for k in range(bases_ref.shape[0]):
            by_y_ref[k, :, dy * block : (dy + 1) * block] = jnp.dot(
                bases_ref[k, :, pl.ds(start, block)], place, preferred_element_type=F32
            ).astype(BF16)
    source = lax.broadcasted_iota(jnp.int32, (ranks, block), 0)
    column = lax.broadcasted_iota(jnp.int32, (ranks, block), 1)
    for dz in range(SIDE):
        wanted = (((column // part) & (SIDE - 1)) * SIDE + dz) * part + (column & (part - 1))
        place = jnp.where(source == wanted, 1.0, 0.0).astype(BF16)
        for k in range(bases_ref.shape[0]):
            by_z_ref[k, :, dz * block : (dz + 1) * block] = jnp.dot(
                by_y_ref[k], place, preferred_element_type=F32
            ).astype(BF16)


def arrange(where, bases, after):
    whole = pl.BlockSpec(bases.shape, lambda i, w: (0, 0, 0))
    return pl.pallas_call(
        arrange_kernel,
        grid_spec=pltpu.PrefetchScalarGridSpec(
            num_scalar_prefetch=1, grid=(1,), in_specs=[whole, ANYWHERE], out_specs=[whole] * 2
        ),
        out_shape=[held(bases.shape)] * 2,
        compiler_params=PARAMS,
        cost_estimate=cost(4 * bases.size * bases.shape[2], 6 * bases.size),
    )(where, bases, after)


def partial_kernel(where_ref, proj_ref, other_proj_ref, grads_ref, other_grads_ref, _, *outs):
    step = pl.program_id(0)
    proj = jnp.concatenate([proj_ref[0], other_proj_ref[0]], axis=0)
    grads = jnp.concatenate([grads_ref[0], other_grads_ref[0]], axis=0)
    total = lax.dot_general(proj, grads, (((0,), (0,)), ((), ())), preferred_element_type=F32)
    span, width = total.shape[1], outs[0].shape[1]
    later = pltpu.roll(total, width, 1)
    total = jnp.where(where_ref[1] == 1, later, total)[:, :width]
    for i, ref in enumerate(outs):

        @pl.when(step == i)
        def _(ref=ref):
            ref[...] = total.astype(ref.dtype)


def partial_grads(where, proj, other_proj, grads, other_grads, which, after):
    _, tokens, rank_part = proj.shape
    pair = grads.shape[2] // SIDE
    width = pair // 2
    span = (width + LANES - 1) // LANES * LANES
    skip = (pair - span) // LANES

    def window(i, w):
        block = (w[0] + i) & (SIDE - 1)
        return which, 0, pl.multiple_of((block * (pair // LANES) + w[1] * skip) * LANES, LANES)

    small = pl.BlockSpec((1, tokens, rank_part), lambda i, w: (which, 0, 0))
    large = pl.BlockSpec((pl.Element(1), pl.Element(tokens), pl.Element(span)), window)
    return pl.pallas_call(
        partial_kernel,
        grid_spec=pltpu.PrefetchScalarGridSpec(
            num_scalar_prefetch=1,
            grid=(SIDE,),
            in_specs=[small, small, large, large, ANYWHERE],
            out_specs=[pl.BlockSpec((rank_part, width), lambda i, w: (0, 0))] * SIDE,
        ),
        out_shape=[held((rank_part, width), F32)] + [held((rank_part, width))] * (SIDE - 1),
        compiler_params=PARAMS,
        cost_estimate=cost(
            4 * tokens * rank_part * width * SIDE, 4 * (tokens + rank_part) * width * SIDE
        ),
    )(where, proj, other_proj, grads, other_grads, after)


def direction_kernel(*refs, pieces):
    own_ref, first_ref, second_ref = refs[0], refs[4], refs[5]
    new_first_ref, new_second_ref = refs[-2 - pieces : -pieces]
    gradient = own_ref[...]
    for ref in refs[1:4]:
        gradient = gradient + ref[...].astype(F32)
    new_first = 0.9 * first_ref[0] + 0.1 * gradient
    new_second = 0.999 * second_ref[0] + 0.001 * gradient * gradient
    new_first_ref[0] = new_first
    new_second_ref[0] = new_second
    first_fix = 1.0 - 0.9**1000.0
    second_fix = 1.0 - 0.999**1000.0
    root = jnp.sqrt(new_second * (1.0 / second_fix)) + 1e-08
    direction = (new_first * (1.0 / first_fix) / root).astype(BF16)
    low = 0
    for ref in refs[-pieces:]:
        size = min(ref.shape[1], direction.shape[1] - low)
        ref[:, :size] = direction[:, low : low + size]
        if size < ref.shape[1]:
            ref[:, size:] = jnp.zeros((ref.shape[0], ref.shape[1] - size), BF16)
        low += size


def directions(own_sum, sums, first_moment, second_moment, which, pieces, before, after):
    _, rows, width = first_moment.shape
    cut = (width // pieces + LANES - 1) // LANES * LANES
    tile = 32
    flat = pl.BlockSpec((tile, width), lambda i: (i, 0))
    own = pl.BlockSpec((1, tile, width), lambda i: (which, i, 0))
    half = pl.BlockSpec((tile, cut), lambda i: (i, 0))
    in_specs = [flat] * SIDE + [own, own]
    args = [own_sum, *sums, first_moment, second_moment]
    aliases = {len(args) + i: i for i in range(len(before))}
    args += [*before, after]
    in_specs += [ANYWHERE] * (len(before) + 1)
    piece = held((rows, cut))
    full = jax.ShapeDtypeStruct(first_moment.shape, F32)
    return pl.pallas_call(
        functools.partial(direction_kernel, pieces=pieces),
        grid=(rows // tile,),
        in_specs=in_specs,
        out_specs=[own, own] + [half] * pieces,
        out_shape=[full, full] + [piece] * pieces,
        input_output_aliases=aliases,
        compiler_params=PARAMS,
        cost_estimate=cost(30 * rows * width, 26 * rows * width),
    )(*args)


def stack_kernel(*refs):
    rows = refs[0].shape[0]
    for i, ref in enumerate(refs[:-1]):
        refs[-1][i * rows : (i + 1) * rows, :] = ref[...]


def stack(pieces):
    rows, width = pieces[0].shape
    return pl.pallas_call(
        stack_kernel,
        out_shape=held((rows * len(pieces), width)),
        compiler_params=PARAMS,
        cost_estimate=cost(0, 4 * rows * width * len(pieces)),
    )(*pieces)


def expand_kernel(*refs, counts, which):
    halves = len(counts)
    out_ref, columns, pieces, outs, in_sems, out_sems = refs[-6:]
    cut = pieces.shape[2]
    loads, refs = [], list(refs)
    for half, count in enumerate(counts):
        loads.append([(refs.pop(0).at[which], columns.at[half])])
        at = 0
        for _ in range(count):
            ref = refs.pop(0)
            loads[half].append((ref, pieces.at[half, pl.ds(at, ref.shape[0])]))
            at += ref.shape[0]
    copies = [
        [pltpu.make_async_copy(a, b, in_sems.at[half, i]) for i, (a, b) in enumerate(group)]
        for half, group in enumerate(loads)
    ]
    for group in copies:
        for copy in group:
            copy.start()
    stores = []
    for half, group in enumerate(copies):
        for copy in group:
            copy.wait()
        outs[half] = lax.dot_general(
            pieces[half], columns[half], (((0,), (1,)), ((), ())), preferred_element_type=F32
        ).astype(BF16)
        size = min(cut, out_ref.shape[1] - half * cut)
        stores.append(
            pltpu.make_async_copy(
                outs.at[half, pl.ds(0, size)],
                out_ref.at[which, pl.ds(half * cut, size)],
                out_sems.at[half],
            )
        )
        stores[-1].start()
    for store in stores:
        store.wait()


def expand_halves(halves, which, width, update):
    count, rows, ranks = halves[0][0].shape
    cut = halves[0][1][0].shape[1]
    counts = tuple(len(pieces) for _, pieces in halves)
    args = [array for columns, pieces in halves for array in (columns, *pieces)]
    aliases = {}
    if update is not None:
        aliases = {len(args): 0}
        args.append(update)
    return pl.pallas_call(
        functools.partial(expand_kernel, counts=counts, which=which),
        in_specs=[ANYWHERE] * len(args),
        out_specs=ANYWHERE,
        out_shape=jax.ShapeDtypeStruct((count, width, rows), BF16),
        scratch_shapes=[
            pltpu.VMEM((len(halves), rows, ranks), BF16),
            pltpu.VMEM((len(halves), ranks, cut), BF16),
            pltpu.VMEM((len(halves), cut, rows), BF16),
            pltpu.SemaphoreType.DMA((len(halves), max(counts) + 1)),
            pltpu.SemaphoreType.DMA((len(halves),)),
        ],
        input_output_aliases=aliases,
        compiler_params=PARAMS,
        cost_estimate=cost(4 * rows * ranks * cut, 4 * (rows * ranks + ranks * cut + rows * cut)),
    )(*args)


def ring_gather(value, first, second, split):
    row = stack([value] + [receive(value, first, d) for d in (1, 2, 3)])
    after = receive(row, second, 1)
    before = receive(row, second, -1)
    if not split:
        return row, after, receive(after, second, 1), before
    half = row.shape[0] // 2
    far_top = receive(after[:half], second, 1)
    far_bottom = receive(before[half:], second, -1)
    return row, after, far_top, far_bottom, before


def on_device(activations, out_grads, bases, first_moment, second_moment):
    where = jnp.stack([lax.axis_index(n) for n in ("x", "c", "y", "z")]).astype(jnp.int32)
    y, z = where[2], where[3]
    features, ranks = bases.shape[1:]
    part = ranks // (SIDE * SIDE)
    width = first_moment.shape[2]

    other_grads = swap_cores(out_grads)

    column = jnp.arange(ranks)
    slow, fast, inner = column // (SIDE * part), column // part % SIDE, column % part
    source = (((y + slow) % SIDE) * SIDE + (z + fast) % SIDE) * part + inner
    place = (column[:, None] == source[None, :]).astype(BF16)
    own = lax.dynamic_slice_in_dim(activations, (y * SIDE + z) * features, features, 1)
    partial = jnp.einsum("td,kdr->ktr", own, bases, preferred_element_type=F32).astype(BF16)
    partial = jnp.einsum("ktr,rs->kts", partial, place, preferred_element_type=F32).astype(BF16)
    for axis in ("y", "z"):
        size = partial.shape[2] // SIDE
        blocks = [partial[:, :, i * size : (i + 1) * size] for i in range(SIDE)]
        total = blocks[0].astype(F32)
        for i in (1, 3, 2):
            total = total + send(blocks[i], axis, i).astype(F32)
        partial = total.astype(BF16)

    other_partial = swap_cores(partial)
    own_sum, *sums = partial_grads(
        where, partial, other_partial, out_grads, other_grads, 0, where
    )
    own_sum_1, *sums_1 = partial_grads(
        where, partial, other_partial, out_grads, other_grads, 1, own_sum
    )
    columns_y, columns_z = arrange(where, bases, own_sum_1)
    sums = [send(value, "x", i + 1) for i, value in enumerate(sums)]
    sums_1 = [send(value, "x", i + 1) for i, value in enumerate(sums_1)]

    moments, update, after = [], None, columns_y
    for which, parts in enumerate(([own_sum, sums], [own_sum_1, sums_1])):
        *moments, left, right = directions(
            *parts, first_moment, second_moment, which, 2, moments, after
        )
        halves = [
            (columns_z, ring_gather(left, "y", "z", which == 1)),
            (columns_y, ring_gather(right, "z", "y", which == 1)),
        ]
        after = halves[0][1][0]
        update = expand_halves(halves, which, width, update)
    return jnp.swapaxes(update, 1, 2), *moments


def solution(mesh):
    grid = Mesh(mesh.devices.reshape(4, 2, 4, 4), ("x", "c", "y", "z"))
    dp, fsdp = ("x", "c"), ("y", "z")
    return jax.shard_map(
        on_device,
        mesh=grid,
        in_specs=(
            P(dp, None),
            P(None, dp, None),
            P(None, fsdp, None),
            P(None, fsdp, dp),
            P(None, fsdp, dp),
        ),
        out_specs=(P(None, fsdp, dp), P(None, fsdp, dp), P(None, fsdp, dp)),
        check_vma=False,
    )
```

```python
import functools

import jax
import jax.numpy as jnp
from jax import lax
from jax.experimental import pallas as pl
from jax.experimental.pallas import tpu as pltpu
from jax.sharding import Mesh, PartitionSpec as P

BF16 = jnp.bfloat16
F32 = jnp.float32
SIDE = 4
LANES = 128
VMEM = 56 * 1024 * 1024
PARAMS = pltpu.CompilerParams(vmem_limit_bytes=VMEM)
ANYWHERE = pl.BlockSpec(memory_space=pl.ANY)


def receive(value, axis, distance):
    return lax.ppermute(value, axis, [((i + distance) % SIDE, i) for i in range(SIDE)])


def send(value, axis, distance):
    return receive(value, axis, -distance)


def swap_cores(value):
    return lax.ppermute(value, "c", [(0, 1), (1, 0)])


def held(shape, dtype=BF16):
    return pltpu.HBM(shape, dtype)


def cost(flops, moved):
    return pl.CostEstimate(flops=flops, bytes_accessed=moved, transcendentals=0)


def arrange_kernel(where_ref, bases_ref, _, by_y_ref, by_z_ref):
    y, z = where_ref[2], where_ref[3]
    ranks = bases_ref.shape[2]
    part = ranks // (SIDE * SIDE)
    block = ranks // SIDE
    source = lax.broadcasted_iota(jnp.int32, (block, block), 0)
    column = lax.broadcasted_iota(jnp.int32, (block, block), 1)
    wanted = ((z + column // part) & (SIDE - 1)) * part + (column & (part - 1))
    place = jnp.where(source == wanted, 1.0, 0.0).astype(BF16)
    for dy in range(SIDE):
        start = pl.multiple_of(((y + dy) & (SIDE - 1)) * block, block)
        for k in range(bases_ref.shape[0]):
            by_y_ref[k, :, dy * block : (dy + 1) * block] = jnp.dot(
                bases_ref[k, :, pl.ds(start, block)], place, preferred_element_type=F32
            ).astype(BF16)
    source = lax.broadcasted_iota(jnp.int32, (ranks, block), 0)
    column = lax.broadcasted_iota(jnp.int32, (ranks, block), 1)
    for dz in range(SIDE):
        wanted = (((column // part) & (SIDE - 1)) * SIDE + dz) * part + (column & (part - 1))
        place = jnp.where(source == wanted, 1.0, 0.0).astype(BF16)
        for k in range(bases_ref.shape[0]):
            by_z_ref[k, :, dz * block : (dz + 1) * block] = jnp.dot(
                by_y_ref[k], place, preferred_element_type=F32
            ).astype(BF16)


def arrange(where, bases, after):
    whole = pl.BlockSpec(bases.shape, lambda i, w: (0, 0, 0))
    return pl.pallas_call(
        arrange_kernel,
        grid_spec=pltpu.PrefetchScalarGridSpec(
            num_scalar_prefetch=1, grid=(1,), in_specs=[whole, ANYWHERE], out_specs=[whole] * 2
        ),
        out_shape=[held(bases.shape)] * 2,
        compiler_params=PARAMS,
        cost_estimate=cost(4 * bases.size * bases.shape[2], 6 * bases.size),
    )(where, bases, after)


def partial_kernel(where_ref, proj_ref, other_proj_ref, grads_ref, other_grads_ref, _, *outs):
    step = pl.program_id(0)
    proj = jnp.concatenate([proj_ref[0], other_proj_ref[0]], axis=0)
    grads = jnp.concatenate([grads_ref[0], other_grads_ref[0]], axis=0)
    total = lax.dot_general(proj, grads, (((0,), (0,)), ((), ())), preferred_element_type=F32)
    span, width = total.shape[1], outs[0].shape[1]
    later = pltpu.roll(total, width, 1)
    total = jnp.where(where_ref[1] == 1, later, total)[:, :width]
    for i, ref in enumerate(outs):

        @pl.when(step == i)
        def _(ref=ref):
            ref[...] = total.astype(ref.dtype)


def partial_grads(where, proj, other_proj, grads, other_grads, which, after):
    _, tokens, rank_part = proj.shape
    pair = grads.shape[2] // SIDE
    width = pair // 2
    span = (width + LANES - 1) // LANES * LANES
    skip = (pair - span) // LANES

    def window(i, w):
        block = (w[0] + i) & (SIDE - 1)
        return which, 0, pl.multiple_of((block * (pair // LANES) + w[1] * skip) * LANES, LANES)

    small = pl.BlockSpec((1, tokens, rank_part), lambda i, w: (which, 0, 0))
    large = pl.BlockSpec((pl.Element(1), pl.Element(tokens), pl.Element(span)), window)
    return pl.pallas_call(
        partial_kernel,
        grid_spec=pltpu.PrefetchScalarGridSpec(
            num_scalar_prefetch=1,
            grid=(SIDE,),
            in_specs=[small, small, large, large, ANYWHERE],
            out_specs=[pl.BlockSpec((rank_part, width), lambda i, w: (0, 0))] * SIDE,
        ),
        out_shape=[held((rank_part, width), F32)] + [held((rank_part, width))] * (SIDE - 1),
        compiler_params=PARAMS,
        cost_estimate=cost(
            4 * tokens * rank_part * width * SIDE, 4 * (tokens + rank_part) * width * SIDE
        ),
    )(where, proj, other_proj, grads, other_grads, after)


def direction_kernel(*refs, pieces):
    own_ref, first_ref, second_ref = refs[0], refs[4], refs[5]
    new_first_ref, new_second_ref = refs[-2 - pieces : -pieces]
    gradient = own_ref[...]
    for ref in refs[1:4]:
        gradient = gradient + ref[...].astype(F32)
    new_first = 0.9 * first_ref[0] + 0.1 * gradient
    new_second = 0.999 * second_ref[0] + 0.001 * gradient * gradient
    new_first_ref[0] = new_first
    new_second_ref[0] = new_second
    first_fix = 1.0 - 0.9**1000.0
    second_fix = 1.0 - 0.999**1000.0
    root = jnp.sqrt(new_second * (1.0 / second_fix)) + 1e-08
    direction = (new_first * (1.0 / first_fix) / root).astype(BF16)
    low = 0
    for ref in refs[-pieces:]:
        size = min(ref.shape[1], direction.shape[1] - low)
        ref[:, :size] = direction[:, low : low + size]
        if size < ref.shape[1]:
            ref[:, size:] = jnp.zeros((ref.shape[0], ref.shape[1] - size), BF16)
        low += size


def directions(own_sum, sums, first_moment, second_moment, which, pieces, before, after):
    _, rows, width = first_moment.shape
    cut = (width // pieces + LANES - 1) // LANES * LANES
    tile = 32
    flat = pl.BlockSpec((tile, width), lambda i: (i, 0))
    own = pl.BlockSpec((1, tile, width), lambda i: (which, i, 0))
    half = pl.BlockSpec((tile, cut), lambda i: (i, 0))
    in_specs = [flat] * SIDE + [own, own]
    args = [own_sum, *sums, first_moment, second_moment]
    aliases = {len(args) + i: i for i in range(len(before))}
    args += [*before, after]
    in_specs += [ANYWHERE] * (len(before) + 1)
    piece = held((rows, cut))
    full = jax.ShapeDtypeStruct(first_moment.shape, F32)
    return pl.pallas_call(
        functools.partial(direction_kernel, pieces=pieces),
        grid=(rows // tile,),
        in_specs=in_specs,
        out_specs=[own, own] + [half] * pieces,
        out_shape=[full, full] + [piece] * pieces,
        input_output_aliases=aliases,
        compiler_params=PARAMS,
        cost_estimate=cost(30 * rows * width, 26 * rows * width),
    )(*args)


def stack_kernel(*refs):
    rows = refs[0].shape[0]
    for i, ref in enumerate(refs[:-1]):
        refs[-1][i * rows : (i + 1) * rows, :] = ref[...]


def stack(pieces):
    rows, width = pieces[0].shape
    return pl.pallas_call(
        stack_kernel,
        out_shape=held((rows * len(pieces), width)),
        compiler_params=PARAMS,
        cost_estimate=cost(0, 4 * rows * width * len(pieces)),
    )(*pieces)


def expand_kernel(*refs, counts, which):
    halves = len(counts)
    out_ref, columns, pieces, outs, in_sems, out_sems = refs[-6:]
    cut = pieces.shape[2]
    loads, refs = [], list(refs)
    for half, count in enumerate(counts):
        loads.append([(refs.pop(0).at[which], columns.at[half])])
        at = 0
        for _ in range(count):
            ref = refs.pop(0)
            loads[half].append((ref, pieces.at[half, pl.ds(at, ref.shape[0])]))
            at += ref.shape[0]
    copies = [
        [pltpu.make_async_copy(a, b, in_sems.at[half, i]) for i, (a, b) in enumerate(group)]
        for half, group in enumerate(loads)
    ]
    for group in copies:
        for copy in group:
            copy.start()
    stores = []
    for half, group in enumerate(copies):
        for copy in group:
            copy.wait()
        outs[half] = lax.dot_general(
            pieces[half], columns[half], (((0,), (1,)), ((), ())), preferred_element_type=F32
        ).astype(BF16)
        size = min(cut, out_ref.shape[1] - half * cut)
        stores.append(
            pltpu.make_async_copy(
                outs.at[half, pl.ds(0, size)],
                out_ref.at[which, pl.ds(half * cut, size)],
                out_sems.at[half],
            )
        )
        stores[-1].start()
    for store in stores:
        store.wait()


def expand_halves(halves, which, width, update):
    count, rows, ranks = halves[0][0].shape
    cut = halves[0][1][0].shape[1]
    counts = tuple(len(pieces) for _, pieces in halves)
    args = [array for columns, pieces in halves for array in (columns, *pieces)]
    aliases = {}
    if update is not None:
        aliases = {len(args): 0}
        args.append(update)
    return pl.pallas_call(
        functools.partial(expand_kernel, counts=counts, which=which),
        in_specs=[ANYWHERE] * len(args),
        out_specs=ANYWHERE,
        out_shape=jax.ShapeDtypeStruct((count, width, rows), BF16),
        scratch_shapes=[
            pltpu.VMEM((len(halves), rows, ranks), BF16),
            pltpu.VMEM((len(halves), ranks, cut), BF16),
            pltpu.VMEM((len(halves), cut, rows), BF16),
            pltpu.SemaphoreType.DMA((len(halves), max(counts) + 1)),
            pltpu.SemaphoreType.DMA((len(halves),)),
        ],
        input_output_aliases=aliases,
        compiler_params=PARAMS,
        cost_estimate=cost(4 * rows * ranks * cut, 4 * (rows * ranks + ranks * cut + rows * cut)),
    )(*args)


def ring_gather(value, first, second, split):
    row = stack([value] + [receive(value, first, d) for d in (1, 2, 3)])
    after = receive(row, second, 1)
    before = receive(row, second, -1)
    if not split:
        return row, after, receive(after, second, 1), before
    half = row.shape[0] // 2
    far_top = receive(after[:half], second, 1)
    far_bottom = receive(before[half:], second, -1)
    return row, after, far_top, far_bottom, before


def on_device(activations, out_grads, bases, first_moment, second_moment):
    where = jnp.stack([lax.axis_index(n) for n in ("x", "c", "y", "z")]).astype(jnp.int32)
    y, z = where[2], where[3]
    features, ranks = bases.shape[1:]
    part = ranks // (SIDE * SIDE)
    width = first_moment.shape[2]

    other_grads = swap_cores(out_grads)

    column = jnp.arange(ranks)
    slow, fast, inner = column // (SIDE * part), column // part % SIDE, column % part
    source = (((y + slow) % SIDE) * SIDE + (z + fast) % SIDE) * part + inner
    place = (column[:, None] == source[None, :]).astype(BF16)
    own = lax.dynamic_slice_in_dim(activations, (y * SIDE + z) * features, features, 1)
    partial = jnp.einsum("td,kdr->ktr", own, bases, preferred_element_type=F32).astype(BF16)
    partial = jnp.einsum("ktr,rs->kts", partial, place, preferred_element_type=F32).astype(BF16)
    for axis in ("y", "z"):
        size = partial.shape[2] // SIDE
        blocks = [partial[:, :, i * size : (i + 1) * size] for i in range(SIDE)]
        total = blocks[0].astype(F32)
        for i in (2, 1, 3):
            total = total + send(blocks[i], axis, i).astype(F32)
        partial = total.astype(BF16)

    other_partial = swap_cores(partial)
    own_sum, *sums = partial_grads(
        where, partial, other_partial, out_grads, other_grads, 0, where
    )
    own_sum_1, *sums_1 = partial_grads(
        where, partial, other_partial, out_grads, other_grads, 1, own_sum
    )
    columns_y, columns_z = arrange(where, bases, own_sum_1)
    sums = [send(value, "x", i + 1) for i, value in enumerate(sums)]
    sums_1 = [send(value, "x", i + 1) for i, value in enumerate(sums_1)]

    moments, update, after = [], None, columns_y
    for which, parts in enumerate(([own_sum, sums], [own_sum_1, sums_1])):
        *moments, left, right = directions(
            *parts, first_moment, second_moment, which, 2, moments, after
        )
        halves = [
            (columns_z, ring_gather(left, "y", "z", which == 1)),
            (columns_y, ring_gather(right, "z", "y", which == 1)),
        ]
        after = halves[0][1][0]
        update = expand_halves(halves, which, width, update)
    return jnp.swapaxes(update, 1, 2), *moments


def solution(mesh):
    grid = Mesh(mesh.devices.reshape(4, 2, 4, 4), ("x", "c", "y", "z"))
    dp, fsdp = ("x", "c"), ("y", "z")
    return jax.shard_map(
        on_device,
        mesh=grid,
        in_specs=(
            P(dp, None),
            P(None, dp, None),
            P(None, fsdp, None),
            P(None, fsdp, dp),
            P(None, fsdp, dp),
        ),
        out_specs=(P(None, fsdp, dp), P(None, fsdp, dp), P(None, fsdp, dp)),
        check_vma=False,
    )
```
